32 devices in a mesh: ens: 2 (over y), gx: 16 (over z, x, core).
Axes of the slice: x: 2, y: 2, z: 4, core: 2. Of those that a mesh axis runs over, the one named last changes fastest.
Arguments:
- pressure_prev: float32 [8, 128, 128], P('ens', 'gx'), parts along dimension 0, may hold values from -2.5 to 2.5
- source: float32 [8, 128, 128], P('ens', 'gx'), parts along dimension 0, may hold values from -8 to 8
- permeability: float32 [8, 128, 128], P('ens', 'gx'), parts along dimension 0, may hold values from 0.3 to 3
- region: int32 [8, 128, 128], P('ens', 'gx'), parts along dimension 0, may hold values from 0 to 7
- region_factor: float32 [16], P('ens'), parts along dimension 0, may hold values from 0.3 to 3
- boundary: int32 [8, 128, 128], P('ens', 'gx'), parts along dimension 0, may hold values from 0 to 2
- flux_prev: float32 [3, 8, 128, 128], P(None, 'ens', 'gx'), parts along dimension 1, may hold values from -2 to 2
- concentration: float32 [4, 8, 128, 128], P(None, 'ens', 'gx'), parts along dimension 1, may hold values from 0.2 to 2
- porosity: float32 [8, 128, 128], P('ens', 'gx'), parts along dimension 0, may hold values from 0.3 to 1
- reaction: float32 [8, 4], P('ens'), parts along dimension 0, may hold values from -3 to 3
Outputs:
- pressure: float32 [8, 128, 128], P('ens', 'gx'), parts along dimension 0
- flux_new: float32 [3, 8, 128, 128], P(None, 'ens', 'gx'), parts along dimension 1
- species_new: float32 [4, 8, 128, 128], P(None, 'ens', 'gx'), parts along dimension 1
The draws below stay inside these ranges and needn't reach their ends.
There are 2 independent parts, one for each index of `ens`. The reference program is written for one: setup_inputs(seed, part) draws one part's arguments, and reference() takes and returns one part's arrays. A program takes and returns all parts, laid end to end along the dimension named above; each array names one. Nothing has to cross between parts.
Inputs may be any that keep to these rules, and one draw needn't show every extreme that they name: Index of the cell's material region into region_factor. 0 inner cell, 1 leaky boundary cell, 2 fixed-pressure well cell.
All inputs are finite; a program needn't handle non-finite values.
Results may differ from the reference program's by a relative error of at most 0.0003.
Values sent between devices are 32-bit elements; how exact they have to be, the bound alone decides.
A program may use at most 64 MiB of HBM per device.

```python
import math
import jax
import jax.numpy as jnp
from jax import lax

LAYERS = 4
SPECIES = 4
REGIONS = 8
ITERS = 2
SUBSTEPS = 2
NX = 128
NY = 128


def draw_source(key, part):
    position = jnp.arange(NX, dtype=jnp.float32) / max(NX - 1, 1)
    rising = (1.0 + 2.0 * position)[None, :, None]
    values = jax.random.normal(key, (LAYERS, NX, NY), jnp.float32) * rising
    return jnp.clip(values, -8.0, 8.0)


def place_ends(drawn, rng, smallest, high):
    longest = drawn.shape.index(max(drawn.shape))
    spots = []
    for shift in (0, 1):
        where = [jax.random.randint(jax.random.fold_in(rng, axis), (), 0, length) for axis, length in enumerate(drawn.shape)]
        where[longest] = (where[longest] + shift) % drawn.shape[longest]
        spots.append(tuple(where))
    return drawn.at[spots[0]].set(smallest).at[spots[1]].set(high)


def block_scale(rng, dims, pieces, smallest, high):
    factor_of = 1.0
    for dim, blocks in pieces:
        draws = jax.random.uniform(jax.random.fold_in(jax.random.fold_in(rng, 6), dim), (blocks,), jnp.float32, smallest / len(pieces), high / len(pieces))
        factor_of = factor_of * jnp.repeat(jnp.exp(draws), dims[dim] // blocks).reshape((-1,) + (1,) * (len(dims) - 1 - dim))
    return factor_of


def bell_draw(own_key, dims, width, reach, split=(), held_as=jnp.bfloat16):
    values = jax.random.normal(own_key, dims, jnp.float32) * width
    if len(split) > 0:
        values = block_scale(own_key, dims, split, -0.22, 0.18) * values
    return jnp.clip(values, min=-reach, max=reach).astype(held_as)


def setup_inputs(seed: int = 0, part: int = 0) -> dict:
    key_of = jax.random.split(jax.random.key(seed), 11)
    part_keys = jax.random.split(jax.random.fold_in(key_of[10], part), 11)
    pressure_prev = bell_draw(part_keys[0], (LAYERS, NX, NY), 0.3, 2.5, ((1, 16),), jnp.float32)
    source = draw_source(jax.random.fold_in(jax.random.fold_in(key_of[10], part), 71), part)
    permeability = jnp.clip(jnp.exp(math.log(3.0) - 2.3025851 * jax.random.uniform(part_keys[2], (LAYERS, NX, NY), jnp.float32) ** block_scale(part_keys[2], (LAYERS, NX, NY), ((1, 16),), -0.2, 0.2)), 0.3, 3.0)
    region = place_ends(jax.random.randint(part_keys[3], (LAYERS, NX, NY), 0, REGIONS), jax.random.fold_in(part_keys[3], 1), 0, REGIONS - 1).astype(jnp.int32)
    region_factor = jnp.clip(jnp.exp(jax.random.uniform(part_keys[4], (REGIONS,), jnp.float32, math.log(0.3), math.log(3.0))), 0.3, 3.0)
    boundary = place_ends(jax.random.randint(part_keys[5], (LAYERS, NX, NY), 0, 3), jax.random.fold_in(part_keys[5], 1), 0, 2).astype(jnp.int32)
    flux_prev = bell_draw(part_keys[6], (3, LAYERS, NX, NY), 0.15, 2.0, ((2, 16),), jnp.float32)
    concentration = jnp.clip(0.2 + 1.8 * jax.random.uniform(part_keys[7], (SPECIES, LAYERS, NY, NX), jnp.float32) ** block_scale(part_keys[7], (SPECIES, LAYERS, NY, NX), ((2, 16),), -0.2, 0.2), 0.2, 2.0)
    porosity = jnp.clip(0.3 + 0.7 * jax.random.uniform(part_keys[8], (LAYERS, NY, NX), jnp.float32) ** block_scale(part_keys[8], (LAYERS, NY, NX), ((1, 16),), -0.2, 0.2), 0.3, 1.0)
    reaction = bell_draw(part_keys[9], (SPECIES, SPECIES), 0.5, 3.0, (), jnp.float32)
    return {"pressure_prev": pressure_prev, "source": source, "permeability": permeability, "region": region, "region_factor": region_factor, "boundary": boundary, "flux_prev": flux_prev, "concentration": concentration, "porosity": porosity, "reaction": reaction}


step_size = 0.5


def harmonic(left_val, right_val):
    return 2.0 * left_val * right_val / (left_val + right_val)


def pad_dim(tensor, along_dim, pad_before, pad_after):
    widths = [(0, 0)] * tensor.ndim
    widths[along_dim] = (pad_before, pad_after)
    return jnp.pad(tensor, widths)


def face_pair(conduct, along_dim):
    length = conduct.shape[along_dim]
    interior = harmonic(lax.slice_in_dim(conduct, 0, length - 1, axis=along_dim), lax.slice_in_dim(conduct, 1, length, axis=along_dim))
    padded = pad_dim(interior, along_dim, 1, 1)
    return lax.slice_in_dim(padded, 0, length, axis=along_dim), lax.slice_in_dim(padded, 1, length + 1, axis=along_dim)


def neighbours(field_in, along_dim):
    length = field_in.shape[along_dim]
    padded = pad_dim(field_in, along_dim, 1, 1)
    return lax.slice_in_dim(padded, 0, length, axis=along_dim), lax.slice_in_dim(padded, 2, length + 2, axis=along_dim)


def operate(field_in, diagonal, trans):
    below_x, above_x = neighbours(field_in, 1)
    below_y, above_y = neighbours(field_in, 2)
    below_z, above_z = neighbours(field_in, 0)
    return diagonal * field_in - (trans[0] * below_x + trans[1] * above_x + trans[2] * below_y + trans[3] * above_y + trans[4] * below_z + trans[5] * above_z)


def advect(species, face_flux, along_dim):
    length = species.shape[along_dim]
    padded = pad_dim(species, along_dim, 0, 1)
    below_cell = lax.slice_in_dim(padded, 0, length, axis=along_dim)
    above_cell = lax.slice_in_dim(padded, 1, length + 1, axis=along_dim)
    carried = face_flux * jnp.where(face_flux > 0, below_cell, above_cell)
    return carried - pad_dim(lax.slice_in_dim(carried, 0, length - 1, axis=along_dim), along_dim, 1, 0)


def reference(pressure_prev, source, permeability, region, region_factor, boundary, flux_prev, concentration, porosity, reaction):
    conduct = region_factor[region] * permeability
    lower_x, upper_x = face_pair(conduct, 1)
    lower_y, upper_y = face_pair(conduct, 2)
    lower_z, upper_z = face_pair(conduct, 0)
    leakage = jnp.where(boundary == 0, 0.05, jnp.where(boundary == 1, 1.0, 10.0)) * conduct
    diagonal = leakage + lower_x + upper_x + lower_y + upper_y + lower_z + upper_z
    trans = (lower_x, upper_x, lower_y, upper_y, lower_z, upper_z)
    pressure = pressure_prev
    residual = source - operate(pressure, diagonal, trans)
    precond = residual / diagonal
    direction = precond
    inner_now = jnp.sum(residual * precond)
    for sweep_index in range(ITERS):
        applied = operate(direction, diagonal, trans)
        step_len = inner_now / jnp.sum(direction * applied)
        pressure = pressure + step_len * direction
        residual = residual - step_len * applied
        precond = residual / diagonal
        inner_next = jnp.sum(residual * precond)
        direction = precond + (inner_next / inner_now) * direction
        inner_now = inner_next
    below_x, above_x = neighbours(pressure, 1)
    below_y, above_y = neighbours(pressure, 2)
    below_z, above_z = neighbours(pressure, 0)
    flux_new = jnp.stack([upper_x * (pressure - above_x), upper_y * (pressure - above_y), upper_z * (pressure - above_z)])
    turned = jnp.transpose(flux_prev, (0, 1, 3, 2))
    face_x = turned[0].at[:, :, -1].set(0.0)
    face_y = turned[1].at[:, -1, :].set(0.0)
    face_z = turned[2].at[-1].set(0.0)
    species = concentration
    for substep in range(SUBSTEPS):
        divergence = advect(species, face_y, 2) + advect(species, face_x, 3) + advect(species, face_z, 1)
        reaction_term = jnp.einsum("st,tzyx->szyx", reaction, species, precision=lax.Precision.HIGHEST)
        species = species - (step_size / porosity) * divergence + step_size * reaction_term
    return pressure, flux_new, species
```

```python
import functools

import jax
import jax.numpy as jnp
from jax import lax
from jax.experimental import pallas as pl
from jax.experimental.pallas import tpu as pltpu
from jax.sharding import PartitionSpec as P

SUBSTEPS = 2
LANES = 128
step_size = 0.5


def harmonic(left_val, right_val):
    return 2.0 * left_val * right_val / (left_val + right_val)


def iota(shape, dim):
    return lax.broadcasted_iota(jnp.int32, shape, dim)


def shift_z(field, by):
    zero = jnp.zeros_like(field[:1])
    if by > 0:
        return jnp.concatenate([field[1:], zero], axis=0)
    return jnp.concatenate([zero, field[:-1]], axis=0)


def next_lane(field):
    return pltpu.roll(field, field.shape[-1] - 1, axis=field.ndim - 1)


def last_lane(field):
    return pltpu.roll(field, 1, axis=field.ndim - 1)


def next_row(field):
    return pltpu.roll(field, field.shape[1] - 1, axis=1)


def last_row(field):
    return pltpu.roll(field, 1, axis=1)


def group_transpose(tiles, width):
    count = len(tiles)
    tiles = list(tiles)
    group = iota(tiles[0].shape, 1) // width
    half = count // 2
    while half:
        low = (group & half) == 0
        for i in range(count):
            if i & half:
                continue
            a, b = tiles[i], tiles[i + half]
            tiles[i] = jnp.where(low, a, pltpu.roll(b, half * width, axis=1))
            tiles[i + half] = jnp.where(low, pltpu.roll(a, LANES - half * width, axis=1), b)
        half //= 2
    return tiles


def kernel(
    peers,
    pres_ref,
    src_ref,
    perm_ref,
    region_ref,
    factor_ref,
    bound_ref,
    flux_ref,
    conc_ref,
    poro_ref,
    react_ref,
    pres_out,
    flux_out,
    spec_out,
    pack_out,
    pack_in,
    edge_out,
    edge_in,
    turn_out,
    turn_in,
    sum_out,
    sum_in,
    pack_ss,
    pack_rs,
    edge_ss,
    edge_rs,
    turn_ss,
    turn_rs,
    sum_ss,
    sum_rs,
):
    me = lax.axis_index("gx")
    layers, rows, ny = pres_ref.shape
    species_n, _, yrows, nx = conc_ref.shape
    has_low = me > 0
    has_high = me < peers - 1

    barrier = pltpu.get_barrier_semaphore()

    def greet(k, carry):
        pl.semaphore_signal(barrier, inc=1, device_id={"gx": lax.rem(me + k, peers)})
        return carry

    lax.fori_loop(1, peers, greet, 0)

    edge_out[0, 0] = conc_ref[:, :, 0:1, :]
    edge_out[0, 1] = conc_ref[:, :, yrows - 1 : yrows, :]

    flux_y = jnp.where(iota((layers, rows, ny), 2) == ny - 1, 0.0, flux_ref[1])
    flux_y_low = last_lane(flux_y)
    turned = jnp.concatenate([flux_ref[0], flux_y, flux_ref[2], flux_y_low], axis=0)
    turned = turned.reshape(4 * layers * rows, ny).T
    turn_out[...] = turned.reshape(peers, yrows, LANES)

    region = region_ref[...]
    factor = jnp.full(region.shape, factor_ref[0], jnp.float32)
    for region_id in range(1, factor_ref.shape[0]):
        factor = jnp.where(region == region_id, factor_ref[region_id], factor)
    conduct = factor * perm_ref[...]
    field = conduct.shape
    row_id = iota(field, 1)
    first_row, end_row = row_id == 0, row_id == rows - 1
    lane_end = iota(field, 2) == ny - 1

    def y_faces(c):
        edge = iota(c.shape, 2) == ny - 1
        return jnp.where(edge, 0.0, harmonic(c, next_lane(c)))

    def z_faces(c):
        zero = jnp.zeros_like(c[:1])
        return jnp.concatenate([harmonic(c[:-1], c[1:]), zero], axis=0)

    ty = y_faces(conduct)
    ty_low = last_lane(ty)
    tz = z_faces(conduct)
    tz_low = shift_z(tz, -1)
    tx = jnp.where(end_row, 0.0, harmonic(conduct, next_row(conduct)))
    tx_low = last_row(tx)
    bound = bound_ref[...]
    leakage = jnp.where(bound == 0, 0.05, jnp.where(bound == 1, 1.0, 10.0)) * conduct
    diag_part = leakage + tx_low + tx + ty_low + ty + tz_low + tz

    def around(f):
        return (
            tx_low * last_row(f)
            + tx * next_row(f)
            + ty_low * last_lane(f)
            + ty * next_lane(f)
            + tz_low * shift_z(f, -1)
            + tz * shift_z(f, 1)
        )

    pres = pres_ref[...]
    res_part = src_ref[...] - (diag_part * pres - around(pres))
    pack_out[0, 0] = conduct[:, 0:1]
    pack_out[0, 1] = pres[:, 0:1]
    pack_out[0, 2] = res_part[:, 0:1]
    pack_out[0, 3] = diag_part[:, 0:1]
    pack_out[0, 4] = res_part[:, 1:2] / diag_part[:, 1:2]
    pack_out[0, 5] = tx[:, 0:1]
    pack_out[1, 0] = conduct[:, rows - 1 : rows]
    pack_out[1, 1] = pres[:, rows - 1 : rows]
    pack_out[1, 2] = res_part[:, rows - 1 : rows]
    pack_out[1, 3] = diag_part[:, rows - 1 : rows]

    pl.semaphore_wait(barrier, peers - 1)

    def to_side(out, into, ss, rs, side):
        return pltpu.make_async_remote_copy(
            src_ref=out,
            dst_ref=into,
            send_sem=ss,
            recv_sem=rs,
            device_id={"gx": me - 1 if side == 0 else me + 1},
        )

    def pack_copy(side):
        used = 6 if side == 0 else 4
        span = pl.ds(0, used)
        return to_side(
            pack_out.at[side, span],
            pack_in.at[1 - side, span],
            pack_ss.at[side],
            pack_rs.at[1 - side],
            side,
        )

    def edge_copy(step, side):
        return to_side(
            edge_out.at[step, side],
            edge_in.at[step, 1 - side],
            edge_ss.at[step, side],
            edge_rs.at[step, 1 - side],
            side,
        )

    def turn_copy(k):
        to = lax.rem(me + k, peers)
        return pltpu.make_async_remote_copy(
            src_ref=turn_out.at[to],
            dst_ref=turn_in.at[me],
            send_sem=turn_ss,
            recv_sem=turn_rs,
            device_id={"gx": to},
        )

    def sum_copy(k):
        to = lax.rem(me + k, peers)
        return pltpu.make_async_remote_copy(
            src_ref=sum_out,
            dst_ref=sum_in.at[me],
            send_sem=sum_ss,
            recv_sem=sum_rs,
            device_id={"gx": to},
        )

    def start_all(copy_of):
        def body(k, carry):
            copy_of(k).start()
            return carry

        lax.fori_loop(1, peers, body, 0)

    def both_sides(copy_of):
        @pl.when(has_low)
        def _():
            copy_of(0).start()

        @pl.when(has_high)
        def _():
            copy_of(1).start()

    def await_sides(copy_of):
        @pl.when(has_low)
        def _():
            copy_of(1).wait_recv()

        @pl.when(has_high)
        def _():
            copy_of(0).wait_recv()

    def sent_sides(copy_of):
        @pl.when(has_low)
        def _():
            copy_of(0).wait_send()

        @pl.when(has_high)
        def _():
            copy_of(1).wait_send()

    def whole(ref_out, ref_in, ss, rs):
        return pltpu.make_async_remote_copy(
            src_ref=ref_out, dst_ref=ref_in, send_sem=ss, recv_sem=rs, device_id={"gx": me}
        )

    both_sides(pack_copy)
    both_sides(functools.partial(edge_copy, 0))
    start_all(turn_copy)
    turn_in[me] = turn_out[me]

    await_sides(pack_copy)
    zero_row = jnp.zeros((layers, 1, ny), jnp.float32)

    def low_of(k):
        return jnp.where(has_low, pack_in[0, k], zero_row)

    def high_of(k):
        return jnp.where(has_high, pack_in[1, k], zero_row)

    one_row = jnp.ones_like(zero_row)
    cond_b = jnp.where(has_low, pack_in[0, 0], one_row)
    cond_a = jnp.where(has_high, pack_in[1, 0], one_row)
    pres_b, pres_a = low_of(1), high_of(1)
    diag_b = jnp.where(has_low, pack_in[0, 3], one_row)
    diag_a = jnp.where(has_high, pack_in[1, 3], one_row)
    t_lo = jnp.where(has_low, harmonic(cond_b, conduct[:, 0:1]), zero_row)
    t_hi = jnp.where(has_high, harmonic(conduct[:, rows - 1 : rows], cond_a), zero_row)
    drop_b = t_lo * (pres_b - pres[:, 0:1])
    drop_a = t_hi * (pres_a - pres[:, rows - 1 : rows])
    z_b = (low_of(2) - drop_b) / (diag_b + t_lo)
    full_a = diag_a + t_hi
    z_a = (high_of(2) - drop_a) / full_a

    zero = jnp.zeros(field, jnp.float32)
    diag = diag_part + jnp.where(first_row, t_lo, zero) + jnp.where(end_row, t_hi, zero)
    res = res_part + jnp.where(first_row, drop_b, zero) + jnp.where(end_row, drop_a, zero)
    z0 = res / diag
    nz = (
        around(z0)
        + jnp.where(first_row, t_lo * z_b, zero)
        + jnp.where(end_row, t_hi * z_a, zero)
    )
    v = nz / diag
    ty_a = y_faces(cond_a)
    tz_a = z_faces(cond_a)
    nz_a = (
        t_hi * z0[:, rows - 1 : rows]
        + high_of(5) * high_of(4)
        + last_lane(ty_a) * last_lane(z_a)
        + ty_a * next_lane(z_a)
        + shift_z(tz_a, -1) * shift_z(z_a, -1)
        + tz_a * shift_z(z_a, 1)
    )
    v_a = nz_a / full_a
    tx_all = jnp.where(end_row, t_hi, tx)
    v_up = tx_all * jnp.where(end_row, v_a, next_row(v)) + ty * next_lane(v) + tz * shift_z(v, 1)

    def column(f):
        f = jnp.sum(jnp.sum(f, axis=0), axis=0, keepdims=True)
        return sum(f[:, i : i + LANES] for i in range(0, ny, LANES))

    columns = (column(res * z0), column(z0 * nz), column(v * nz), column(2.0 * (v * v_up)))
    sum_row = iota((8, LANES), 0)
    partial = jnp.zeros((8, LANES), jnp.float32)
    for k, col in enumerate(columns):
        partial = jnp.where(sum_row == k, col, partial)
    sum_out[...] = partial
    start_all(sum_copy)
    sum_in[me] = partial

    some = pl.ds(0, peers - 1)
    whole(turn_out.at[some], turn_in.at[some], turn_ss, turn_rs).wait_recv()
    await_sides(functools.partial(edge_copy, 0))
    per = LANES // rows
    blocks = [
        group_transpose([turn_in[b * per + i] for i in range(per)], rows)
        for b in range(peers // per)
    ]

    def component(c):
        def layer(z):
            parts = [block[c * layers + z] for block in blocks]
            return parts[0] if len(parts) == 1 else jnp.concatenate(parts, axis=1)

        return jnp.stack([layer(z) for z in range(layers)])

    shape = (layers, yrows, nx)
    y_first, y_end = iota(shape, 1) == 0, iota(shape, 1) == yrows - 1
    f_x = jnp.where(iota(shape, 2) == nx - 1, 0.0, component(0))
    f_y = component(1)
    f_z = jnp.where(iota(shape, 0) == layers - 1, 0.0, component(2))
    f_y_low = component(3)
    up_x, up_y, up_z, up_y_low = f_x > 0, f_y > 0, f_z > 0, f_y_low > 0
    weight = step_size / poro_ref[...]
    edge_zero = jnp.zeros((layers, 1, nx), jnp.float32)

    def advance(species, step):
        result = []
        for s in range(species_n):
            c = species[s]
            below = jnp.where(has_low, edge_in[step, 0, s], edge_zero)
            above = jnp.where(has_high, edge_in[step, 1, s], edge_zero)
            c_below = jnp.where(y_first, below, last_row(c))
            c_above = jnp.where(y_end, above, next_row(c))
            div = f_y * jnp.where(up_y, c, c_above) - f_y_low * jnp.where(up_y_low, c_below, c)
            carried = f_x * jnp.where(up_x, c, next_lane(c))
            div = div + (carried - last_lane(carried))
            carried = f_z * jnp.where(up_z, c, shift_z(c, 1))
            div = div + (carried - shift_z(carried, -1))
            react = react_ref[s, 0] * species[0]
            for t in range(1, species_n):
                react = react + react_ref[s, t] * species[t]
            result.append(c - weight * div + step_size * react)
        return result

    species = advance([conc_ref[s] for s in range(species_n)], 0)
    for s in range(species_n):
        edge_out[1, 0, s] = species[s][:, 0:1]
        edge_out[1, 1, s] = species[s][:, yrows - 1 : yrows]
    both_sides(functools.partial(edge_copy, 1))

    whole(sum_in.at[some], sum_in.at[some], sum_ss, sum_rs).wait_recv()
    total = sum_in[0]
    for i in range(1, peers):
        total = total + sum_in[i]
    total = jnp.sum(total, axis=1, keepdims=True)
    g00, g01, g11, g12 = (total[k : k + 1] for k in range(4))
    delta0 = g00 - g01
    a0 = g00 / delta0
    e0 = -g01 / delta0
    gamma1 = e0 * e0 * g00 + 2.0 * a0 * e0 * g01 + a0 * a0 * g11
    cross1 = e0 * e0 * g01 + 2.0 * a0 * e0 * g11 + a0 * a0 * g12
    beta = gamma1 / g00
    a1 = gamma1 / ((gamma1 - cross1) - beta * gamma1 / a0)
    on_z = (a0 + a1 * (e0 + beta)).reshape(1, 1, 1)
    on_v = (a1 * a0).reshape(1, 1, 1)
    pressure = pres + on_z * z0 + on_v * v
    pressure_a = pres_a + on_z * z_a + on_v * v_a
    pres_out[...] = pressure
    flux_out[0] = tx_all * (pressure - jnp.where(end_row, pressure_a, next_row(pressure)))
    flux_out[1] = ty * (pressure - next_lane(pressure))
    flux_out[2] = tz * (pressure - shift_z(pressure, 1))

    await_sides(functools.partial(edge_copy, 1))
    species = advance(species, 1)
    for s in range(species_n):
        spec_out[s] = species[s]

    sent_sides(pack_copy)
    sent_sides(functools.partial(edge_copy, 0))
    sent_sides(functools.partial(edge_copy, 1))
    whole(turn_out.at[some], turn_in.at[some], turn_ss, turn_rs).wait_send()
    whole(sum_in.at[some], sum_in.at[some], sum_ss, sum_rs).wait_send()


def solution(mesh):
    peers = mesh.shape["gx"]

    def step(pres, src, perm, region, factor, bound, flux, conc, poro, react):
        layers, rows, ny = pres.shape
        species_n, _, yrows, nx = conc.shape
        vmem = pl.BlockSpec(memory_space=pltpu.VMEM)
        smem = pl.BlockSpec(memory_space=pltpu.SMEM)
        f32 = jnp.float32
        dma = pltpu.SemaphoreType.DMA
        return pl.pallas_call(
            functools.partial(kernel, peers),
            out_shape=(
                jax.ShapeDtypeStruct(pres.shape, f32),
                jax.ShapeDtypeStruct(flux.shape, f32),
                jax.ShapeDtypeStruct(conc.shape, f32),
            ),
            in_specs=[vmem, vmem, vmem, vmem, smem, vmem, vmem, vmem, vmem, smem],
            out_specs=(vmem, vmem, vmem),
            scratch_shapes=[
                pltpu.VMEM((2, 6, layers, 1, ny), f32),
                pltpu.VMEM((2, 6, layers, 1, ny), f32),
                pltpu.VMEM((SUBSTEPS, 2, species_n, layers, 1, nx), f32),
                pltpu.VMEM((SUBSTEPS, 2, species_n, layers, 1, nx), f32),
                pltpu.VMEM((peers, yrows, LANES), f32),
                pltpu.VMEM((peers, yrows, LANES), f32),
                pltpu.VMEM((8, LANES), f32),
                pltpu.VMEM((peers, 8, LANES), f32),
                dma((2,)),
                dma((2,)),
                dma((SUBSTEPS, 2)),
                dma((SUBSTEPS, 2)),
                dma,
                dma,
                dma,
                dma,
            ],
            compiler_params=pltpu.CompilerParams(
                collective_id=0, has_side_effects=True, vmem_limit_bytes=24 * 1024 * 1024
            ),
        )(pres, src, perm, region, factor, bound, flux, conc, poro, react)

    slab = P("ens", "gx", None)
    stacked = P(None, "ens", "gx", None)
    in_specs = (slab, slab, slab, slab, P("ens"), slab, stacked, stacked, slab, P("ens", None))
    out_specs = (slab, stacked, stacked)
    return jax.shard_map(step, mesh=mesh, in_specs=in_specs, out_specs=out_specs, check_vma=False)
```

```python
import functools

import jax
import jax.numpy as jnp
from jax import lax
from jax.experimental import pallas as pl
from jax.experimental.pallas import tpu as pltpu
from jax.sharding import PartitionSpec as P

SUBSTEPS = 2
LANES = 128
VMEM_GRANT = 60 * 1024 * 1024
step_size = 0.5


def harmonic(left_val, right_val):
    return 2.0 * left_val * right_val / (left_val + right_val)


def iota(shape, dim):
    return lax.broadcasted_iota(jnp.int32, shape, dim)


def shift_z(field, by):
    zero = jnp.zeros_like(field[:1])
    if by > 0:
        return jnp.concatenate([field[1:], zero], axis=0)
    return jnp.concatenate([zero, field[:-1]], axis=0)


def next_lane(field):
    return pltpu.roll(field, field.shape[-1] - 1, axis=field.ndim - 1)


def last_lane(field):
    return pltpu.roll(field, 1, axis=field.ndim - 1)


def next_row(field):
    return pltpu.roll(field, field.shape[1] - 1, axis=1)


def last_row(field):
    return pltpu.roll(field, 1, axis=1)


def group_transpose(tiles, width):
    count = len(tiles)
    tiles = list(tiles)
    group = iota(tiles[0].shape, 1) // width
    half = count // 2
    while half:
        low = (group & half) == 0
        for i in range(count):
            if i & half:
                continue
            a, b = tiles[i], tiles[i + half]
            tiles[i] = jnp.where(low, a, pltpu.roll(b, half * width, axis=1))
            tiles[i + half] = jnp.where(low, pltpu.roll(a, LANES - half * width, axis=1), b)
        half //= 2
    return tiles


def kernel(
    peers,
    pres_hbm,
    src_hbm,
    perm_hbm,
    region_hbm,
    factor_hbm,
    bound_hbm,
    flux_hbm,
    conc_hbm,
    poro_hbm,
    react_hbm,
    pres_out_hbm,
    flux_out_hbm,
    spec_out_hbm,
    pres_ref,
    src_ref,
    perm_ref,
    region_ref,
    factor_ref,
    bound_ref,
    flux_ref,
    conc_ref,
    poro_ref,
    react_ref,
    load_sem,
    pres_out,
    flux_out,
    spec_out,
    store_sem,
    pack_out,
    pack_in,
    edge_out,
    edge_in,
    turn_out,
    turn_in,
    sum_out,
    sum_in,
    pack_ss,
    pack_rs,
    edge_ss,
    edge_rs,
    turn_ss,
    turn_rs,
    sum_ss,
    sum_rs,
):
    me = lax.axis_index("gx")
    layers, rows, ny = pres_ref.shape
    species_n, _, yrows, nx = conc_ref.shape
    has_low = me > 0
    has_high = me < peers - 1

    barrier = pltpu.get_barrier_semaphore()

    def greet(k, carry):
        pl.semaphore_signal(barrier, inc=1, device_id={"gx": lax.rem(me + k, peers)})
        return carry

    lax.fori_loop(1, peers, greet, 0)

    pairs = (
        (region_hbm, region_ref),
        (factor_hbm, factor_ref),
        (perm_hbm, perm_ref),
        (bound_hbm, bound_ref),
        (pres_hbm, pres_ref),
        (src_hbm, src_ref),
        (flux_hbm, flux_ref),
        (conc_hbm, conc_ref),
        (poro_hbm, poro_ref),
        (react_hbm, react_ref),
    )
    loads = [pltpu.make_async_copy(a, b, load_sem.at[i]) for i, (a, b) in enumerate(pairs)]
    for load in loads:
        load.start()
    for load in loads[:6]:
        load.wait()

    region = region_ref[...]
    factor = jnp.full(region.shape, factor_ref[0], jnp.float32)
    for region_id in range(1, factor_ref.shape[0]):
        factor = jnp.where(region == region_id, factor_ref[region_id], factor)
    conduct = factor * perm_ref[...]
    field = conduct.shape
    row_id = iota(field, 1)
    first_row, end_row = row_id == 0, row_id == rows - 1
    lane_end = iota(field, 2) == ny - 1

    def y_faces(c):
        edge = iota(c.shape, 2) == ny - 1
        return jnp.where(edge, 0.0, harmonic(c, next_lane(c)))

    def z_faces(c):
        zero = jnp.zeros_like(c[:1])
        return jnp.concatenate([harmonic(c[:-1], c[1:]), zero], axis=0)

    ty = y_faces(conduct)
    ty_low = last_lane(ty)
    tz = z_faces(conduct)
    tz_low = shift_z(tz, -1)
    tx = jnp.where(end_row, 0.0, harmonic(conduct, next_row(conduct)))
    tx_low = last_row(tx)
    bound = bound_ref[...]
    leakage = jnp.where(bound == 0, 0.05, jnp.where(bound == 1, 1.0, 10.0)) * conduct
    diag_part = leakage + tx_low + tx + ty_low + ty + tz_low + tz

    def around(f):
        return (
            tx_low * last_row(f)
            + tx * next_row(f)
            + ty_low * last_lane(f)
            + ty * next_lane(f)
            + tz_low * shift_z(f, -1)
            + tz * shift_z(f, 1)
        )

    pres = pres_ref[...]
    res_part = src_ref[...] - (diag_part * pres - around(pres))
    pack_out[0, 0] = conduct[:, 0:1]
    pack_out[0, 1] = pres[:, 0:1]
    pack_out[0, 2] = res_part[:, 0:1]
    pack_out[0, 3] = diag_part[:, 0:1]
    pack_out[0, 4] = res_part[:, 1:2] / diag_part[:, 1:2]
    pack_out[0, 5] = tx[:, 0:1]
    pack_out[1, 0] = conduct[:, rows - 1 : rows]
    pack_out[1, 1] = pres[:, rows - 1 : rows]
    pack_out[1, 2] = res_part[:, rows - 1 : rows]
    pack_out[1, 3] = diag_part[:, rows - 1 : rows]

    pl.semaphore_wait(barrier, peers - 1)

    def to_side(out, into, ss, rs, side):
        return pltpu.make_async_remote_copy(
            src_ref=out,
            dst_ref=into,
            send_sem=ss,
            recv_sem=rs,
            device_id={"gx": me - 1 if side == 0 else me + 1},
        )

    def pack_copy(side):
        used = 6 if side == 0 else 4
        span = pl.ds(0, used)
        return to_side(
            pack_out.at[side, span],
            pack_in.at[1 - side, span],
            pack_ss.at[side],
            pack_rs.at[1 - side],
            side,
        )

    def edge_copy(step, side):
        return to_side(
            edge_out.at[step, side],
            edge_in.at[step, 1 - side],
            edge_ss.at[step, side],
            edge_rs.at[step, 1 - side],
            side,
        )

    def turn_copy(k):
        to = lax.rem(me + k, peers)
        return pltpu.make_async_remote_copy(
            src_ref=turn_out.at[to],
            dst_ref=turn_in.at[me],
            send_sem=turn_ss,
            recv_sem=turn_rs,
            device_id={"gx": to},
        )

    def sum_copy(k):
        to = lax.rem(me + k, peers)
        return pltpu.make_async_remote_copy(
            src_ref=sum_out,
            dst_ref=sum_in.at[me],
            send_sem=sum_ss,
            recv_sem=sum_rs,
            device_id={"gx": to},
        )

    def start_all(copy_of):
        def body(k, carry):
            copy_of(k).start()
            return carry

        lax.fori_loop(1, peers, body, 0)

    def both_sides(copy_of):
        @pl.when(has_low)
        def _():
            copy_of(0).start()

        @pl.when(has_high)
        def _():
            copy_of(1).start()

    def await_sides(copy_of):
        @pl.when(has_low)
        def _():
            copy_of(1).wait_recv()

        @pl.when(has_high)
        def _():
            copy_of(0).wait_recv()

    def sent_sides(copy_of):
        @pl.when(has_low)
        def _():
            copy_of(0).wait_send()

        @pl.when(has_high)
        def _():
            copy_of(1).wait_send()

    def whole(ref_out, ref_in, ss, rs):
        return pltpu.make_async_remote_copy(
            src_ref=ref_out, dst_ref=ref_in, send_sem=ss, recv_sem=rs, device_id={"gx": me}
        )

    both_sides(pack_copy)
    for load in loads[6:]:
        load.wait()
    edge_out[0, 0] = conc_ref[:, :, 0:1, :]
    edge_out[0, 1] = conc_ref[:, :, yrows - 1 : yrows, :]

    flux_y = jnp.where(iota((layers, rows, ny), 2) == ny - 1, 0.0, flux_ref[1])
    flux_y_low = last_lane(flux_y)
    turned = jnp.concatenate([flux_ref[0], flux_y, flux_ref[2], flux_y_low], axis=0)
    turned = turned.reshape(4 * layers * rows, ny).T
    turn_out[...] = turned.reshape(peers, yrows, LANES)
    both_sides(functools.partial(edge_copy, 0))
    start_all(turn_copy)
    turn_in[me] = turn_out[me]

    await_sides(pack_copy)
    zero_row = jnp.zeros((layers, 1, ny), jnp.float32)

    def low_of(k):
        return jnp.where(has_low, pack_in[0, k], zero_row)

    def high_of(k):
        return jnp.where(has_high, pack_in[1, k], zero_row)

    one_row = jnp.ones_like(zero_row)
    cond_b = jnp.where(has_low, pack_in[0, 0], one_row)
    cond_a = jnp.where(has_high, pack_in[1, 0], one_row)
    pres_b, pres_a = low_of(1), high_of(1)
    diag_b = jnp.where(has_low, pack_in[0, 3], one_row)
    diag_a = jnp.where(has_high, pack_in[1, 3], one_row)
    t_lo = jnp.where(has_low, harmonic(cond_b, conduct[:, 0:1]), zero_row)
    t_hi = jnp.where(has_high, harmonic(conduct[:, rows - 1 : rows], cond_a), zero_row)
    drop_b = t_lo * (pres_b - pres[:, 0:1])
    drop_a = t_hi * (pres_a - pres[:, rows - 1 : rows])
    z_b = (low_of(2) - drop_b) / (diag_b + t_lo)
    full_a = diag_a + t_hi
    z_a = (high_of(2) - drop_a) / full_a

    zero = jnp.zeros(field, jnp.float32)
    diag = diag_part + jnp.where(first_row, t_lo, zero) + jnp.where(end_row, t_hi, zero)
    res = res_part + jnp.where(first_row, drop_b, zero) + jnp.where(end_row, drop_a, zero)
    z0 = res / diag
    nz = (
        around(z0)
        + jnp.where(first_row, t_lo * z_b, zero)
        + jnp.where(end_row, t_hi * z_a, zero)
    )
    v = nz / diag
    ty_a = y_faces(cond_a)
    tz_a = z_faces(cond_a)
    nz_a = (
        t_hi * z0[:, rows - 1 : rows]
        + high_of(5) * high_of(4)
        + last_lane(ty_a) * last_lane(z_a)
        + ty_a * next_lane(z_a)
        + shift_z(tz_a, -1) * shift_z(z_a, -1)
        + tz_a * shift_z(z_a, 1)
    )
    v_a = nz_a / full_a
    tx_all = jnp.where(end_row, t_hi, tx)
    v_up = tx_all * jnp.where(end_row, v_a, next_row(v)) + ty * next_lane(v) + tz * shift_z(v, 1)

    def column(f):
        f = jnp.sum(jnp.sum(f, axis=0), axis=0, keepdims=True)
        return sum(f[:, i : i + LANES] for i in range(0, ny, LANES))

    columns = (column(res * z0), column(z0 * nz), column(v * nz), column(2.0 * (v * v_up)))
    sum_row = iota((8, LANES), 0)
    partial = jnp.zeros((8, LANES), jnp.float32)
    for k, col in enumerate(columns):
        partial = jnp.where(sum_row == k, col, partial)
    sum_out[...] = partial
    start_all(sum_copy)
    sum_in[me] = partial

    some = pl.ds(0, peers - 1)
    whole(turn_out.at[some], turn_in.at[some], turn_ss, turn_rs).wait_recv()
    await_sides(functools.partial(edge_copy, 0))
    per = LANES // rows
    blocks = [
        group_transpose([turn_in[b * per + i] for i in range(per)], rows)
        for b in range(peers // per)
    ]

    def component(c):
        def layer(z):
            parts = [block[c * layers + z] for block in blocks]
            return parts[0] if len(parts) == 1 else jnp.concatenate(parts, axis=1)

        return jnp.stack([layer(z) for z in range(layers)])

    shape = (layers, yrows, nx)
    y_first, y_end = iota(shape, 1) == 0, iota(shape, 1) == yrows - 1
    f_x = jnp.where(iota(shape, 2) == nx - 1, 0.0, component(0))
    f_y = component(1)
    f_z = jnp.where(iota(shape, 0) == layers - 1, 0.0, component(2))
    f_y_low = component(3)
    up_x, up_y, up_z, up_y_low = f_x > 0, f_y > 0, f_z > 0, f_y_low > 0
    weight = step_size / poro_ref[...]
    edge_zero = jnp.zeros((layers, 1, nx), jnp.float32)

    def advance(species, step):
        result = []
        for s in range(species_n):
            c = species[s]
            below = jnp.where(has_low, edge_in[step, 0, s], edge_zero)
            above = jnp.where(has_high, edge_in[step, 1, s], edge_zero)
            c_below = jnp.where(y_first, below, last_row(c))
            c_above = jnp.where(y_end, above, next_row(c))
            div = f_y * jnp.where(up_y, c, c_above) - f_y_low * jnp.where(up_y_low, c_below, c)
            carried = f_x * jnp.where(up_x, c, next_lane(c))
            div = div + (carried - last_lane(carried))
            carried = f_z * jnp.where(up_z, c, shift_z(c, 1))
            div = div + (carried - shift_z(carried, -1))
            react = react_ref[s, 0] * species[0]
            for t in range(1, species_n):
                react = react + react_ref[s, t] * species[t]
            result.append(c - weight * div + step_size * react)
        return result

    species = advance([conc_ref[s] for s in range(species_n)], 0)
    for s in range(species_n):
        edge_out[1, 0, s] = species[s][:, 0:1]
        edge_out[1, 1, s] = species[s][:, yrows - 1 : yrows]
    both_sides(functools.partial(edge_copy, 1))

    whole(sum_in.at[some], sum_in.at[some], sum_ss, sum_rs).wait_recv()
    total = sum_in[0]
    for i in range(1, peers):
        total = total + sum_in[i]
    total = jnp.sum(total, axis=1, keepdims=True)
    g00, g01, g11, g12 = (total[k : k + 1] for k in range(4))
    delta0 = g00 - g01
    a0 = g00 / delta0
    e0 = -g01 / delta0
    gamma1 = e0 * e0 * g00 + 2.0 * a0 * e0 * g01 + a0 * a0 * g11
    cross1 = e0 * e0 * g01 + 2.0 * a0 * e0 * g11 + a0 * a0 * g12
    beta = gamma1 / g00
    a1 = gamma1 / ((gamma1 - cross1) - beta * gamma1 / a0)
    on_z = (a0 + a1 * (e0 + beta)).reshape(1, 1, 1)
    on_v = (a1 * a0).reshape(1, 1, 1)
    pressure = pres + on_z * z0 + on_v * v
    pressure_a = pres_a + on_z * z_a + on_v * v_a
    pres_out[...] = pressure
    flux_out[0] = tx_all * (pressure - jnp.where(end_row, pressure_a, next_row(pressure)))
    flux_out[1] = ty * (pressure - next_lane(pressure))
    flux_out[2] = tz * (pressure - shift_z(pressure, 1))

    stores = [
        pltpu.make_async_copy(pres_out, pres_out_hbm, store_sem.at[0]),
        pltpu.make_async_copy(flux_out, flux_out_hbm, store_sem.at[1]),
        pltpu.make_async_copy(spec_out, spec_out_hbm, store_sem.at[2]),
    ]
    stores[0].start()
    stores[1].start()

    await_sides(functools.partial(edge_copy, 1))
    species = advance(species, 1)
    for s in range(species_n):
        spec_out[s] = species[s]
    stores[2].start()

    sent_sides(pack_copy)
    sent_sides(functools.partial(edge_copy, 0))
    sent_sides(functools.partial(edge_copy, 1))
    whole(turn_out.at[some], turn_in.at[some], turn_ss, turn_rs).wait_send()
    whole(sum_in.at[some], sum_in.at[some], sum_ss, sum_rs).wait_send()
    for store in stores:
        store.wait()


def write_out(a, b, c, a_out, b_out, c_out, sem):
    pairs = ((c, c_out), (b, b_out), (a, a_out))
    copies = [pltpu.make_async_copy(x, y, sem.at[i]) for i, (x, y) in enumerate(pairs)]
    for copy in copies:
        copy.start()
    for copy in copies:
        copy.wait()


def solution(mesh):
    peers = mesh.shape["gx"]

    def step(pres, src, perm, region, factor, bound, flux, conc, poro, react):
        layers, rows, ny = pres.shape
        species_n, _, yrows, nx = conc.shape
        f32 = jnp.float32
        dma = pltpu.SemaphoreType.DMA
        hbm = pl.BlockSpec(memory_space=pltpu.HBM)
        outs = pl.pallas_call(
            functools.partial(kernel, peers),
            out_shape=(
                jax.ShapeDtypeStruct(pres.shape, f32),
                jax.ShapeDtypeStruct(flux.shape, f32),
                jax.ShapeDtypeStruct(conc.shape, f32),
            ),
            in_specs=[hbm] * 10,
            out_specs=(hbm,) * 3,
            scratch_shapes=[
                pltpu.VMEM(pres.shape, f32),
                pltpu.VMEM(pres.shape, f32),
                pltpu.VMEM(pres.shape, f32),
                pltpu.VMEM(pres.shape, jnp.int32),
                pltpu.SMEM(factor.shape, f32),
                pltpu.VMEM(pres.shape, jnp.int32),
                pltpu.VMEM(flux.shape, f32),
                pltpu.VMEM(conc.shape, f32),
                pltpu.VMEM(poro.shape, f32),
                pltpu.SMEM(react.shape, f32),
                dma((10,)),
                pltpu.VMEM(pres.shape, f32),
                pltpu.VMEM(flux.shape, f32),
                pltpu.VMEM(conc.shape, f32),
                dma((3,)),
                pltpu.VMEM((2, 6, layers, 1, ny), f32),
                pltpu.VMEM((2, 6, layers, 1, ny), f32),
                pltpu.VMEM((SUBSTEPS, 2, species_n, layers, 1, nx), f32),
                pltpu.VMEM((SUBSTEPS, 2, species_n, layers, 1, nx), f32),
                pltpu.VMEM((peers, yrows, LANES), f32),
                pltpu.VMEM((peers, yrows, LANES), f32),
                pltpu.VMEM((8, LANES), f32),
                pltpu.VMEM((peers, 8, LANES), f32),
                dma((2,)),
                dma((2,)),
                dma((SUBSTEPS, 2)),
                dma((SUBSTEPS, 2)),
                dma,
                dma,
                dma,
                dma,
            ],
            compiler_params=pltpu.CompilerParams(
                collective_id=0, has_side_effects=True, vmem_limit_bytes=VMEM_GRANT
            ),
        )(pres, src, perm, region, factor, bound, flux, conc, poro, react)
        return pl.pallas_call(
            write_out,
            out_shape=tuple(jax.ShapeDtypeStruct(o.shape, f32) for o in outs),
            in_specs=[hbm] * 3,
            out_specs=(hbm,) * 3,
            scratch_shapes=[dma((3,))],
            compiler_params=pltpu.CompilerParams(vmem_limit_bytes=VMEM_GRANT),
        )(*outs)

    slab = P("ens", "gx", None)
    stacked = P(None, "ens", "gx", None)
    in_specs = (slab, slab, slab, slab, P("ens"), slab, stacked, stacked, slab, P("ens", None))
    out_specs = (slab, stacked, stacked)
    return jax.shard_map(step, mesh=mesh, in_specs=in_specs, out_specs=out_specs, check_vma=False)
```

```python
import functools

import jax
import jax.numpy as jnp
from jax import lax
from jax.experimental import pallas as pl
from jax.experimental.pallas import tpu as pltpu
from jax.sharding import PartitionSpec as P

SUBSTEPS = 2
LANES = 128
VMEM_GRANT = 60 * 1024 * 1024
step_size = 0.5


def harmonic(left_val, right_val):
    return 2.0 * left_val * right_val / (left_val + right_val)


def iota(shape, dim):
    return lax.broadcasted_iota(jnp.int32, shape, dim)


def shift_z(field, by):
    zero = jnp.zeros_like(field[:1])
    if by > 0:
        return jnp.concatenate([field[1:], zero], axis=0)
    return jnp.concatenate([zero, field[:-1]], axis=0)


def next_lane(field):
    return pltpu.roll(field, field.shape[-1] - 1, axis=field.ndim - 1)


def last_lane(field):
    return pltpu.roll(field, 1, axis=field.ndim - 1)


def next_row(field):
    return pltpu.roll(field, field.shape[1] - 1, axis=1)


def last_row(field):
    return pltpu.roll(field, 1, axis=1)


def group_transpose(tiles, width):
    count = len(tiles)
    tiles = list(tiles)
    group = iota(tiles[0].shape, 1) // width
    half = count // 2
    while half:
        low = (group & half) == 0
        for i in range(count):
            if i & half:
                continue
            a, b = tiles[i], tiles[i + half]
            tiles[i] = jnp.where(low, a, pltpu.roll(b, half * width, axis=1))
            tiles[i + half] = jnp.where(low, pltpu.roll(a, LANES - half * width, axis=1), b)
        half //= 2
    return tiles


def kernel(
    peers,
    pres_hbm,
    src_hbm,
    perm_hbm,
    region_hbm,
    factor_hbm,
    bound_hbm,
    flux_hbm,
    conc_hbm,
    poro_hbm,
    react_hbm,
    pres_out_hbm,
    flux_out_hbm,
    spec_out_hbm,
    pres_ref,
    src_ref,
    perm_ref,
    region_ref,
    factor_ref,
    bound_ref,
    flux_ref,
    conc_ref,
    poro_ref,
    react_ref,
    load_sem,
    pres_out,
    flux_out,
    spec_out,
    store_sem,
    pack_out,
    pack_in,
    edge_out,
    edge_in,
    turn_out,
    turn_in,
    sum_out,
    sum_in,
    pack_ss,
    pack_rs,
    edge_ss,
    edge_rs,
    turn_ss,
    turn_rs,
    sum_ss,
    sum_rs,
):
    me = lax.axis_index("gx")
    layers, rows, ny = pres_ref.shape
    species_n, _, yrows, nx = conc_ref.shape
    has_low = me > 0
    has_high = me < peers - 1

    barrier = pltpu.get_barrier_semaphore()

    def greet(k, carry):
        pl.semaphore_signal(barrier, inc=1, device_id={"gx": lax.rem(me + k, peers)})
        return carry

    lax.fori_loop(1, peers, greet, 0)

    pairs = (
        (region_hbm, region_ref),
        (factor_hbm, factor_ref),
        (perm_hbm, perm_ref),
        (bound_hbm, bound_ref),
        (pres_hbm, pres_ref),
        (src_hbm, src_ref),
        (flux_hbm, flux_ref),
        (conc_hbm, conc_ref),
        (poro_hbm, poro_ref),
        (react_hbm, react_ref),
    )
    loads = [pltpu.make_async_copy(a, b, load_sem.at[i]) for i, (a, b) in enumerate(pairs)]
    for load in loads:
        load.start()
    for load in loads[:6]:
        load.wait()

    region = region_ref[...]
    factor = jnp.full(region.shape, factor_ref[0], jnp.float32)
    for region_id in range(1, factor_ref.shape[0]):
        factor = jnp.where(region == region_id, factor_ref[region_id], factor)
    conduct = factor * perm_ref[...]
    field = conduct.shape
    row_id = iota(field, 1)
    first_row, end_row = row_id == 0, row_id == rows - 1
    lane_end = iota(field, 2) == ny - 1

    def y_faces(c):
        edge = iota(c.shape, 2) == ny - 1
        return jnp.where(edge, 0.0, harmonic(c, next_lane(c)))

    def z_faces(c):
        zero = jnp.zeros_like(c[:1])
        return jnp.concatenate([harmonic(c[:-1], c[1:]), zero], axis=0)

    ty = y_faces(conduct)
    ty_low = last_lane(ty)
    tz = z_faces(conduct)
    tz_low = shift_z(tz, -1)
    tx = jnp.where(end_row, 0.0, harmonic(conduct, next_row(conduct)))
    tx_low = last_row(tx)
    bound = bound_ref[...]
    leakage = jnp.where(bound == 0, 0.05, jnp.where(bound == 1, 1.0, 10.0)) * conduct
    diag_part = leakage + tx_low + tx + ty_low + ty + tz_low + tz

    def around(f):
        return (
            tx_low * last_row(f)
            + tx * next_row(f)
            + ty_low * last_lane(f)
            + ty * next_lane(f)
            + tz_low * shift_z(f, -1)
            + tz * shift_z(f, 1)
        )

    pres = pres_ref[...]
    res_part = src_ref[...] - (diag_part * pres - around(pres))
    pack_out[0, 0] = conduct[:, 0:1]
    pack_out[0, 1] = pres[:, 0:1]
    pack_out[0, 2] = res_part[:, 0:1]
    pack_out[0, 3] = diag_part[:, 0:1]
    pack_out[0, 4] = res_part[:, 1:2] / diag_part[:, 1:2]
    pack_out[0, 5] = tx[:, 0:1]
    pack_out[1, 0] = conduct[:, rows - 1 : rows]
    pack_out[1, 1] = pres[:, rows - 1 : rows]
    pack_out[1, 2] = res_part[:, rows - 1 : rows]
    pack_out[1, 3] = diag_part[:, rows - 1 : rows]

    pl.semaphore_wait(barrier, peers - 1)

    def to_side(out, into, ss, rs, side):
        return pltpu.make_async_remote_copy(
            src_ref=out,
            dst_ref=into,
            send_sem=ss,
            recv_sem=rs,
            device_id={"gx": me - 1 if side == 0 else me + 1},
        )

    def pack_copy(side):
        used = 6 if side == 0 else 4
        span = pl.ds(0, used)
        return to_side(
            pack_out.at[side, span],
            pack_in.at[1 - side, span],
            pack_ss.at[side],
            pack_rs.at[1 - side],
            side,
        )

    def edge_copy(step, side):
        return to_side(
            edge_out.at[step, side],
            edge_in.at[step, 1 - side],
            edge_ss.at[step, side],
            edge_rs.at[step, 1 - side],
            side,
        )

    def turn_copy(k):
        to = lax.rem(me + k, peers)
        return pltpu.make_async_remote_copy(
            src_ref=turn_out.at[to],
            dst_ref=turn_in.at[me],
            send_sem=turn_ss,
            recv_sem=turn_rs,
            device_id={"gx": to},
        )

    def sum_copy(k):
        to = lax.rem(me + k, peers)
        return pltpu.make_async_remote_copy(
            src_ref=sum_out,
            dst_ref=sum_in.at[me],
            send_sem=sum_ss,
            recv_sem=sum_rs,
            device_id={"gx": to},
        )

    def start_all(copy_of):
        def body(k, carry):
            copy_of(k).start()
            return carry

        lax.fori_loop(1, peers, body, 0)

    def both_sides(copy_of):
        @pl.when(has_low)
        def _():
            copy_of(0).start()

        @pl.when(has_high)
        def _():
            copy_of(1).start()

    def await_sides(copy_of):
        @pl.when(has_low)
        def _():
            copy_of(1).wait_recv()

        @pl.when(has_high)
        def _():
            copy_of(0).wait_recv()

    def sent_sides(copy_of):
        @pl.when(has_low)
        def _():
            copy_of(0).wait_send()

        @pl.when(has_high)
        def _():
            copy_of(1).wait_send()

    def whole(ref_out, ref_in, ss, rs):
        return pltpu.make_async_remote_copy(
            src_ref=ref_out, dst_ref=ref_in, send_sem=ss, recv_sem=rs, device_id={"gx": me}
        )

    both_sides(pack_copy)
    for load in loads[6:]:
        load.wait()
    edge_out[0, 0] = conc_ref[:, :, 0:1, :]
    edge_out[0, 1] = conc_ref[:, :, yrows - 1 : yrows, :]

    flux_y = jnp.where(iota((layers, rows, ny), 2) == ny - 1, 0.0, flux_ref[1])
    flux_y_low = last_lane(flux_y)
    turned = jnp.concatenate([flux_ref[0], flux_y, flux_ref[2], flux_y_low], axis=0)
    turned = turned.reshape(4 * layers * rows, ny).T
    turn_out[...] = turned.reshape(peers, yrows, LANES)
    both_sides(functools.partial(edge_copy, 0))
    start_all(turn_copy)
    turn_in[me] = turn_out[me]

    await_sides(pack_copy)
    zero_row = jnp.zeros((layers, 1, ny), jnp.float32)

    def low_of(k):
        return jnp.where(has_low, pack_in[0, k], zero_row)

    def high_of(k):
        return jnp.where(has_high, pack_in[1, k], zero_row)

    one_row = jnp.ones_like(zero_row)
    cond_b = jnp.where(has_low, pack_in[0, 0], one_row)
    cond_a = jnp.where(has_high, pack_in[1, 0], one_row)
    pres_b, pres_a = low_of(1), high_of(1)
    diag_b = jnp.where(has_low, pack_in[0, 3], one_row)
    diag_a = jnp.where(has_high, pack_in[1, 3], one_row)
    t_lo = jnp.where(has_low, harmonic(cond_b, conduct[:, 0:1]), zero_row)
    t_hi = jnp.where(has_high, harmonic(conduct[:, rows - 1 : rows], cond_a), zero_row)
    drop_b = t_lo * (pres_b - pres[:, 0:1])
    drop_a = t_hi * (pres_a - pres[:, rows - 1 : rows])
    z_b = (low_of(2) - drop_b) / (diag_b + t_lo)
    full_a = diag_a + t_hi
    z_a = (high_of(2) - drop_a) / full_a

    zero = jnp.zeros(field, jnp.float32)
    diag = diag_part + jnp.where(first_row, t_lo, zero) + jnp.where(end_row, t_hi, zero)
    res = res_part + jnp.where(first_row, drop_b, zero) + jnp.where(end_row, drop_a, zero)
    z0 = res / diag
    nz = (
        around(z0)
        + jnp.where(first_row, t_lo * z_b, zero)
        + jnp.where(end_row, t_hi * z_a, zero)
    )
    v = nz / diag
    ty_a = y_faces(cond_a)
    tz_a = z_faces(cond_a)
    nz_a = (
        t_hi * z0[:, rows - 1 : rows]
        + high_of(5) * high_of(4)
        + last_lane(ty_a) * last_lane(z_a)
        + ty_a * next_lane(z_a)
        + shift_z(tz_a, -1) * shift_z(z_a, -1)
        + tz_a * shift_z(z_a, 1)
    )
    v_a = nz_a / full_a
    tx_all = jnp.where(end_row, t_hi, tx)
    v_up = tx_all * jnp.where(end_row, v_a, next_row(v)) + ty * next_lane(v) + tz * shift_z(v, 1)

    def column(f):
        f = jnp.sum(jnp.sum(f, axis=0), axis=0, keepdims=True)
        return sum(f[:, i : i + LANES] for i in range(0, ny, LANES))

    columns = (column(res * z0), column(z0 * nz), column(v * nz), column(2.0 * (v * v_up)))
    sum_row = iota((8, LANES), 0)
    partial = jnp.zeros((8, LANES), jnp.float32)
    for k, col in enumerate(columns):
        partial = jnp.where(sum_row == k, col, partial)
    sum_out[...] = partial
    start_all(sum_copy)
    sum_in[me] = partial

    some = pl.ds(0, peers - 1)
    whole(turn_out.at[some], turn_in.at[some], turn_ss, turn_rs).wait_recv()
    await_sides(functools.partial(edge_copy, 0))
    per = LANES // rows
    blocks = [
        group_transpose([turn_in[b * per + i] for i in range(per)], rows)
        for b in range(peers // per)
    ]

    def component(c):
        def layer(z):
            parts = [block[c * layers + z] for block in blocks]
            return parts[0] if len(parts) == 1 else jnp.concatenate(parts, axis=1)

        return jnp.stack([layer(z) for z in range(layers)])

    shape = (layers, yrows, nx)
    y_first, y_end = iota(shape, 1) == 0, iota(shape, 1) == yrows - 1
    f_x = jnp.where(iota(shape, 2) == nx - 1, 0.0, component(0))
    f_y = component(1)
    f_z = jnp.where(iota(shape, 0) == layers - 1, 0.0, component(2))
    f_y_low = component(3)
    up_x, up_y, up_z, up_y_low = f_x > 0, f_y > 0, f_z > 0, f_y_low > 0
    weight = step_size / poro_ref[...]
    edge_zero = jnp.zeros((layers, 1, nx), jnp.float32)

    def advance(species, step):
        result = []
        for s in range(species_n):
            c = species[s]
            below = jnp.where(has_low, edge_in[step, 0, s], edge_zero)
            above = jnp.where(has_high, edge_in[step, 1, s], edge_zero)
            c_below = jnp.where(y_first, below, last_row(c))
            c_above = jnp.where(y_end, above, next_row(c))
            div = f_y * jnp.where(up_y, c, c_above) - f_y_low * jnp.where(up_y_low, c_below, c)
            carried = f_x * jnp.where(up_x, c, next_lane(c))
            div = div + (carried - last_lane(carried))
            carried = f_z * jnp.where(up_z, c, shift_z(c, 1))
            div = div + (carried - shift_z(carried, -1))
            react = react_ref[s, 0] * species[0]
            for t in range(1, species_n):
                react = react + react_ref[s, t] * species[t]
            result.append(c - weight * div + step_size * react)
        return result

    species = advance([conc_ref[s] for s in range(species_n)], 0)
    for s in range(species_n):
        edge_out[1, 0, s] = species[s][:, 0:1]
        edge_out[1, 1, s] = species[s][:, yrows - 1 : yrows]
    both_sides(functools.partial(edge_copy, 1))

    whole(sum_in.at[some], sum_in.at[some], sum_ss, sum_rs).wait_recv()
    total = sum_in[0]
    for i in range(1, peers):
        total = total + sum_in[i]
    total = jnp.sum(total, axis=1, keepdims=True)
    g00, g01, g11, g12 = (total[k : k + 1] for k in range(4))
    delta0 = g00 - g01
    a0 = g00 / delta0
    e0 = -g01 / delta0
    gamma1 = e0 * e0 * g00 + 2.0 * a0 * e0 * g01 + a0 * a0 * g11
    cross1 = e0 * e0 * g01 + 2.0 * a0 * e0 * g11 + a0 * a0 * g12
    beta = gamma1 / g00
    a1 = gamma1 / ((gamma1 - cross1) - beta * gamma1 / a0)
    on_z = (a0 + a1 * (e0 + beta)).reshape(1, 1, 1)
    on_v = (a1 * a0).reshape(1, 1, 1)
    pressure = pres + on_z * z0 + on_v * v
    pressure_a = pres_a + on_z * z_a + on_v * v_a
    pres_out[...] = pressure
    flux_out[0] = tx_all * (pressure - jnp.where(end_row, pressure_a, next_row(pressure)))
    flux_out[1] = ty * (pressure - next_lane(pressure))
    flux_out[2] = tz * (pressure - shift_z(pressure, 1))

    stores = [
        pltpu.make_async_copy(pres_out, pres_out_hbm, store_sem.at[0]),
        pltpu.make_async_copy(flux_out, flux_out_hbm, store_sem.at[1]),
        pltpu.make_async_copy(spec_out, spec_out_hbm, store_sem.at[2]),
    ]
    stores[0].start()
    stores[1].start()

    await_sides(functools.partial(edge_copy, 1))
    species = advance(species, 1)
    for s in range(species_n):
        spec_out[s] = species[s]
    stores[2].start()

    sent_sides(pack_copy)
    sent_sides(functools.partial(edge_copy, 0))
    sent_sides(functools.partial(edge_copy, 1))
    whole(turn_out.at[some], turn_in.at[some], turn_ss, turn_rs).wait_send()
    whole(sum_in.at[some], sum_in.at[some], sum_ss, sum_rs).wait_send()
    for store in stores:
        store.wait()


def solution(mesh):
    peers = mesh.shape["gx"]

    def step(pres, src, perm, region, factor, bound, flux, conc, poro, react):
        layers, rows, ny = pres.shape
        species_n, _, yrows, nx = conc.shape
        f32 = jnp.float32
        dma = pltpu.SemaphoreType.DMA
        hbm = pl.BlockSpec(memory_space=pltpu.HBM)
        outs = pl.pallas_call(
            functools.partial(kernel, peers),
            out_shape=(
                jax.ShapeDtypeStruct(pres.shape, f32),
                jax.ShapeDtypeStruct(flux.shape, f32),
                jax.ShapeDtypeStruct(conc.shape, f32),
            ),
            in_specs=[hbm] * 10,
            out_specs=(hbm,) * 3,
            scratch_shapes=[
                pltpu.VMEM(pres.shape, f32),
                pltpu.VMEM(pres.shape, f32),
                pltpu.VMEM(pres.shape, f32),
                pltpu.VMEM(pres.shape, jnp.int32),
                pltpu.SMEM(factor.shape, f32),
                pltpu.VMEM(pres.shape, jnp.int32),
                pltpu.VMEM(flux.shape, f32),
                pltpu.VMEM(conc.shape, f32),
                pltpu.VMEM(poro.shape, f32),
                pltpu.SMEM(react.shape, f32),
                dma((10,)),
                pltpu.VMEM(pres.shape, f32),
                pltpu.VMEM(flux.shape, f32),
                pltpu.VMEM(conc.shape, f32),
                dma((3,)),
                pltpu.VMEM((2, 6, layers, 1, ny), f32),
                pltpu.VMEM((2, 6, layers, 1, ny), f32),
                pltpu.VMEM((SUBSTEPS, 2, species_n, layers, 1, nx), f32),
                pltpu.VMEM((SUBSTEPS, 2, species_n, layers, 1, nx), f32),
                pltpu.VMEM((peers, yrows, LANES), f32),
                pltpu.VMEM((peers, yrows, LANES), f32),
                pltpu.VMEM((8, LANES), f32),
                pltpu.VMEM((peers, 8, LANES), f32),
                dma((2,)),
                dma((2,)),
                dma((SUBSTEPS, 2)),
                dma((SUBSTEPS, 2)),
                dma,
                dma,
                dma,
                dma,
            ],
            compiler_params=pltpu.CompilerParams(
                collective_id=0, has_side_effects=True, vmem_limit_bytes=VMEM_GRANT
            ),
        )(pres, src, perm, region, factor, bound, flux, conc, poro, react)
        return outs

    slab = P("ens", "gx", None)
    stacked = P(None, "ens", "gx", None)
    in_specs = (slab, slab, slab, slab, P("ens"), slab, stacked, stacked, slab, P("ens", None))
    out_specs = (slab, stacked, stacked)
    return jax.shard_map(step, mesh=mesh, in_specs=in_specs, out_specs=out_specs, check_vma=False)
```

```python
import functools

import jax
import jax.numpy as jnp
from jax import lax
from jax.experimental import pallas as pl
from jax.experimental.pallas import tpu as pltpu
from jax.sharding import PartitionSpec as P

SUBSTEPS = 2
LANES = 128
VMEM_GRANT = 24 * 1024 * 1024
step_size = 0.5


def harmonic(left_val, right_val):
    return 2.0 * left_val * right_val / (left_val + right_val)


def iota(shape, dim):
    return lax.broadcasted_iota(jnp.int32, shape, dim)


def shift_z(field, by):
    zero = jnp.zeros_like(field[:1])
    if by > 0:
        return jnp.concatenate([field[1:], zero], axis=0)
    return jnp.concatenate([zero, field[:-1]], axis=0)


def next_lane(field):
    return pltpu.roll(field, field.shape[-1] - 1, axis=field.ndim - 1)


def last_lane(field):
    return pltpu.roll(field, 1, axis=field.ndim - 1)


def next_row(field):
    return pltpu.roll(field, field.shape[1] - 1, axis=1)


def last_row(field):
    return pltpu.roll(field, 1, axis=1)


def group_transpose(tiles, width):
    count = len(tiles)
    tiles = list(tiles)
    group = iota(tiles[0].shape, 1) // width
    half = count // 2
    while half:
        low = (group & half) == 0
        for i in range(count):
            if i & half:
                continue
            a, b = tiles[i], tiles[i + half]
            tiles[i] = jnp.where(low, a, pltpu.roll(b, half * width, axis=1))
            tiles[i + half] = jnp.where(low, pltpu.roll(a, LANES - half * width, axis=1), b)
        half //= 2
    return tiles


def kernel(
    peers,
    pres_hbm,
    src_hbm,
    perm_hbm,
    region_hbm,
    factor_hbm,
    bound_hbm,
    flux_hbm,
    conc_hbm,
    poro_hbm,
    react_hbm,
    pres_out,
    flux_out,
    spec_out,
    pres_ref,
    src_ref,
    perm_ref,
    region_ref,
    factor_ref,
    bound_ref,
    flux_ref,
    conc_ref,
    poro_ref,
    react_ref,
    load_sem,
    pack_out,
    pack_in,
    edge_out,
    edge_in,
    turn_out,
    turn_in,
    sum_out,
    sum_in,
    pack_ss,
    pack_rs,
    edge_ss,
    edge_rs,
    turn_ss,
    turn_rs,
    sum_ss,
    sum_rs,
):
    me = lax.axis_index("gx")
    layers, rows, ny = pres_ref.shape
    species_n, _, yrows, nx = conc_ref.shape
    has_low = me > 0
    has_high = me < peers - 1

    barrier = pltpu.get_barrier_semaphore()

    def greet(k, carry):
        pl.semaphore_signal(barrier, inc=1, device_id={"gx": lax.rem(me + k, peers)})
        return carry

    lax.fori_loop(1, peers, greet, 0)

    pairs = (
        (region_hbm, region_ref),
        (factor_hbm, factor_ref),
        (perm_hbm, perm_ref),
        (bound_hbm, bound_ref),
        (pres_hbm, pres_ref),
        (src_hbm, src_ref),
        (flux_hbm, flux_ref),
        (conc_hbm, conc_ref),
        (poro_hbm, poro_ref),
        (react_hbm, react_ref),
    )
    loads = [pltpu.make_async_copy(a, b, load_sem.at[i]) for i, (a, b) in enumerate(pairs)]
    for load in loads:
        load.start()
    for load in loads[:6]:
        load.wait()

    region = region_ref[...]
    factor = jnp.full(region.shape, factor_ref[0], jnp.float32)
    for region_id in range(1, factor_ref.shape[0]):
        factor = jnp.where(region == region_id, factor_ref[region_id], factor)
    conduct = factor * perm_ref[...]
    field = conduct.shape
    row_id = iota(field, 1)
    first_row, end_row = row_id == 0, row_id == rows - 1
    lane_end = iota(field, 2) == ny - 1

    def y_faces(c):
        edge = iota(c.shape, 2) == ny - 1
        return jnp.where(edge, 0.0, harmonic(c, next_lane(c)))

    def z_faces(c):
        zero = jnp.zeros_like(c[:1])
        return jnp.concatenate([harmonic(c[:-1], c[1:]), zero], axis=0)

    ty = y_faces(conduct)
    ty_low = last_lane(ty)
    tz = z_faces(conduct)
    tz_low = shift_z(tz, -1)
    tx = jnp.where(end_row, 0.0, harmonic(conduct, next_row(conduct)))
    tx_low = last_row(tx)
    bound = bound_ref[...]
    leakage = jnp.where(bound == 0, 0.05, jnp.where(bound == 1, 1.0, 10.0)) * conduct
    diag_part = leakage + tx_low + tx + ty_low + ty + tz_low + tz

    def around(f):
        return (
            tx_low * last_row(f)
            + tx * next_row(f)
            + ty_low * last_lane(f)
            + ty * next_lane(f)
            + tz_low * shift_z(f, -1)
            + tz * shift_z(f, 1)
        )

    pres = pres_ref[...]
    res_part = src_ref[...] - (diag_part * pres - around(pres))
    pack_out[0, 0] = conduct[:, 0:1]
    pack_out[0, 1] = pres[:, 0:1]
    pack_out[0, 2] = res_part[:, 0:1]
    pack_out[0, 3] = diag_part[:, 0:1]
    pack_out[0, 4] = res_part[:, 1:2] / diag_part[:, 1:2]
    pack_out[0, 5] = tx[:, 0:1]
    pack_out[1, 0] = conduct[:, rows - 1 : rows]
    pack_out[1, 1] = pres[:, rows - 1 : rows]
    pack_out[1, 2] = res_part[:, rows - 1 : rows]
    pack_out[1, 3] = diag_part[:, rows - 1 : rows]

    pl.semaphore_wait(barrier, peers - 1)

    def to_side(out, into, ss, rs, side):
        return pltpu.make_async_remote_copy(
            src_ref=out,
            dst_ref=into,
            send_sem=ss,
            recv_sem=rs,
            device_id={"gx": me - 1 if side == 0 else me + 1},
        )

    def pack_copy(side):
        used = 6 if side == 0 else 4
        span = pl.ds(0, used)
        return to_side(
            pack_out.at[side, span],
            pack_in.at[1 - side, span],
            pack_ss.at[side],
            pack_rs.at[1 - side],
            side,
        )

    def edge_copy(step, side):
        return to_side(
            edge_out.at[step, side],
            edge_in.at[step, 1 - side],
            edge_ss.at[step, side],
            edge_rs.at[step, 1 - side],
            side,
        )

    def turn_copy(k):
        to = lax.rem(me + k, peers)
        return pltpu.make_async_remote_copy(
            src_ref=turn_out.at[to],
            dst_ref=turn_in.at[me],
            send_sem=turn_ss,
            recv_sem=turn_rs,
            device_id={"gx": to},
        )

    def sum_copy(k):
        to = lax.rem(me + k, peers)
        return pltpu.make_async_remote_copy(
            src_ref=sum_out,
            dst_ref=sum_in.at[me],
            send_sem=sum_ss,
            recv_sem=sum_rs,
            device_id={"gx": to},
        )

    def start_all(copy_of):
        def body(k, carry):
            copy_of(k).start()
            return carry

        lax.fori_loop(1, peers, body, 0)

    def both_sides(copy_of):
        @pl.when(has_low)
        def _():
            copy_of(0).start()

        @pl.when(has_high)
        def _():
            copy_of(1).start()

    def await_sides(copy_of):
        @pl.when(has_low)
        def _():
            copy_of(1).wait_recv()

        @pl.when(has_high)
        def _():
            copy_of(0).wait_recv()

    def sent_sides(copy_of):
        @pl.when(has_low)
        def _():
            copy_of(0).wait_send()

        @pl.when(has_high)
        def _():
            copy_of(1).wait_send()

    def whole(ref_out, ref_in, ss, rs):
        return pltpu.make_async_remote_copy(
            src_ref=ref_out, dst_ref=ref_in, send_sem=ss, recv_sem=rs, device_id={"gx": me}
        )

    both_sides(pack_copy)
    for load in loads[6:]:
        load.wait()
    edge_out[0, 0] = conc_ref[:, :, 0:1, :]
    edge_out[0, 1] = conc_ref[:, :, yrows - 1 : yrows, :]

    flux_y = jnp.where(iota((layers, rows, ny), 2) == ny - 1, 0.0, flux_ref[1])
    flux_y_low = last_lane(flux_y)
    turned = jnp.concatenate([flux_ref[0], flux_y, flux_ref[2], flux_y_low], axis=0)
    turned = turned.reshape(4 * layers * rows, ny).T
    turn_out[...] = turned.reshape(peers, yrows, LANES)
    both_sides(functools.partial(edge_copy, 0))
    start_all(turn_copy)
    turn_in[me] = turn_out[me]

    await_sides(pack_copy)
    zero_row = jnp.zeros((layers, 1, ny), jnp.float32)

    def low_of(k):
        return jnp.where(has_low, pack_in[0, k], zero_row)

    def high_of(k):
        return jnp.where(has_high, pack_in[1, k], zero_row)

    one_row = jnp.ones_like(zero_row)
    cond_b = jnp.where(has_low, pack_in[0, 0], one_row)
    cond_a = jnp.where(has_high, pack_in[1, 0], one_row)
    pres_b, pres_a = low_of(1), high_of(1)
    diag_b = jnp.where(has_low, pack_in[0, 3], one_row)
    diag_a = jnp.where(has_high, pack_in[1, 3], one_row)
    t_lo = jnp.where(has_low, harmonic(cond_b, conduct[:, 0:1]), zero_row)
    t_hi = jnp.where(has_high, harmonic(conduct[:, rows - 1 : rows], cond_a), zero_row)
    drop_b = t_lo * (pres_b - pres[:, 0:1])
    drop_a = t_hi * (pres_a - pres[:, rows - 1 : rows])
    z_b = (low_of(2) - drop_b) / (diag_b + t_lo)
    full_a = diag_a + t_hi
    z_a = (high_of(2) - drop_a) / full_a

    zero = jnp.zeros(field, jnp.float32)
    diag = diag_part + jnp.where(first_row, t_lo, zero) + jnp.where(end_row, t_hi, zero)
    res = res_part + jnp.where(first_row, drop_b, zero) + jnp.where(end_row, drop_a, zero)
    z0 = res / diag
    nz = (
        around(z0)
        + jnp.where(first_row, t_lo * z_b, zero)
        + jnp.where(end_row, t_hi * z_a, zero)
    )
    v = nz / diag
    ty_a = y_faces(cond_a)
    tz_a = z_faces(cond_a)
    nz_a = (
        t_hi * z0[:, rows - 1 : rows]
        + high_of(5) * high_of(4)
        + last_lane(ty_a) * last_lane(z_a)
        + ty_a * next_lane(z_a)
        + shift_z(tz_a, -1) * shift_z(z_a, -1)
        + tz_a * shift_z(z_a, 1)
    )
    v_a = nz_a / full_a
    tx_all = jnp.where(end_row, t_hi, tx)
    v_up = tx_all * jnp.where(end_row, v_a, next_row(v)) + ty * next_lane(v) + tz * shift_z(v, 1)

    def column(f):
        f = jnp.sum(jnp.sum(f, axis=0), axis=0, keepdims=True)
        return sum(f[:, i : i + LANES] for i in range(0, ny, LANES))

    columns = (column(res * z0), column(z0 * nz), column(v * nz), column(2.0 * (v * v_up)))
    sum_row = iota((8, LANES), 0)
    partial = jnp.zeros((8, LANES), jnp.float32)
    for k, col in enumerate(columns):
        partial = jnp.where(sum_row == k, col, partial)
    sum_out[...] = partial
    start_all(sum_copy)
    sum_in[me] = partial

    some = pl.ds(0, peers - 1)
    whole(turn_out.at[some], turn_in.at[some], turn_ss, turn_rs).wait_recv()
    await_sides(functools.partial(edge_copy, 0))
    per = LANES // rows
    blocks = [
        group_transpose([turn_in[b * per + i] for i in range(per)], rows)
        for b in range(peers // per)
    ]

    def component(c):
        def layer(z):
            parts = [block[c * layers + z] for block in blocks]
            return parts[0] if len(parts) == 1 else jnp.concatenate(parts, axis=1)

        return jnp.stack([layer(z) for z in range(layers)])

    shape = (layers, yrows, nx)
    y_first, y_end = iota(shape, 1) == 0, iota(shape, 1) == yrows - 1
    f_x = jnp.where(iota(shape, 2) == nx - 1, 0.0, component(0))
    f_y = component(1)
    f_z = jnp.where(iota(shape, 0) == layers - 1, 0.0, component(2))
    f_y_low = component(3)
    up_x, up_y, up_z, up_y_low = f_x > 0, f_y > 0, f_z > 0, f_y_low > 0
    weight = step_size / poro_ref[...]
    edge_zero = jnp.zeros((layers, 1, nx), jnp.float32)

    def advance(species, step):
        result = []
        for s in range(species_n):
            c = species[s]
            below = jnp.where(has_low, edge_in[step, 0, s], edge_zero)
            above = jnp.where(has_high, edge_in[step, 1, s], edge_zero)
            c_below = jnp.where(y_first, below, last_row(c))
            c_above = jnp.where(y_end, above, next_row(c))
            div = f_y * jnp.where(up_y, c, c_above) - f_y_low * jnp.where(up_y_low, c_below, c)
            carried = f_x * jnp.where(up_x, c, next_lane(c))
            div = div + (carried - last_lane(carried))
            carried = f_z * jnp.where(up_z, c, shift_z(c, 1))
            div = div + (carried - shift_z(carried, -1))
            react = react_ref[s, 0] * species[0]
            for t in range(1, species_n):
                react = react + react_ref[s, t] * species[t]
            result.append(c - weight * div + step_size * react)
        return result

    species = advance([conc_ref[s] for s in range(species_n)], 0)
    for s in range(species_n):
        edge_out[1, 0, s] = species[s][:, 0:1]
        edge_out[1, 1, s] = species[s][:, yrows - 1 : yrows]
    both_sides(functools.partial(edge_copy, 1))

    whole(sum_in.at[some], sum_in.at[some], sum_ss, sum_rs).wait_recv()
    total = sum_in[0]
    for i in range(1, peers):
        total = total + sum_in[i]
    total = jnp.sum(total, axis=1, keepdims=True)
    g00, g01, g11, g12 = (total[k : k + 1] for k in range(4))
    delta0 = g00 - g01
    a0 = g00 / delta0
    e0 = -g01 / delta0
    gamma1 = e0 * e0 * g00 + 2.0 * a0 * e0 * g01 + a0 * a0 * g11
    cross1 = e0 * e0 * g01 + 2.0 * a0 * e0 * g11 + a0 * a0 * g12
    beta = gamma1 / g00
    a1 = gamma1 / ((gamma1 - cross1) - beta * gamma1 / a0)
    on_z = (a0 + a1 * (e0 + beta)).reshape(1, 1, 1)
    on_v = (a1 * a0).reshape(1, 1, 1)
    pressure = pres + on_z * z0 + on_v * v
    pressure_a = pres_a + on_z * z_a + on_v * v_a
    pres_out[...] = pressure
    flux_out[0] = tx_all * (pressure - jnp.where(end_row, pressure_a, next_row(pressure)))
    flux_out[1] = ty * (pressure - next_lane(pressure))
    flux_out[2] = tz * (pressure - shift_z(pressure, 1))

    await_sides(functools.partial(edge_copy, 1))
    species = advance(species, 1)
    for s in range(species_n):
        spec_out[s] = species[s]

    sent_sides(pack_copy)
    sent_sides(functools.partial(edge_copy, 0))
    sent_sides(functools.partial(edge_copy, 1))
    whole(turn_out.at[some], turn_in.at[some], turn_ss, turn_rs).wait_send()
    whole(sum_in.at[some], sum_in.at[some], sum_ss, sum_rs).wait_send()


def solution(mesh):
    peers = mesh.shape["gx"]

    def step(pres, src, perm, region, factor, bound, flux, conc, poro, react):
        layers, rows, ny = pres.shape
        species_n, _, yrows, nx = conc.shape
        f32 = jnp.float32
        dma = pltpu.SemaphoreType.DMA
        inputs = (pres, src, perm, region, factor, bound, flux, conc, poro, react)
        hbm = pl.BlockSpec(memory_space=pltpu.HBM)
        vmem = pl.BlockSpec(memory_space=pltpu.VMEM)
        outs = pl.pallas_call(
            functools.partial(kernel, peers),
            out_shape=(
                jax.ShapeDtypeStruct(pres.shape, f32),
                jax.ShapeDtypeStruct(flux.shape, f32),
                jax.ShapeDtypeStruct(conc.shape, f32),
            ),
            in_specs=[hbm] * 10,
            out_specs=(vmem,) * 3,
            scratch_shapes=[
                pltpu.VMEM(pres.shape, f32),
                pltpu.VMEM(pres.shape, f32),
                pltpu.VMEM(pres.shape, f32),
                pltpu.VMEM(pres.shape, jnp.int32),
                pltpu.SMEM(factor.shape, f32),
                pltpu.VMEM(pres.shape, jnp.int32),
                pltpu.VMEM(flux.shape, f32),
                pltpu.VMEM(conc.shape, f32),
                pltpu.VMEM(poro.shape, f32),
                pltpu.SMEM(react.shape, f32),
                dma((10,)),
                pltpu.VMEM((2, 6, layers, 1, ny), f32),
                pltpu.VMEM((2, 6, layers, 1, ny), f32),
                pltpu.VMEM((SUBSTEPS, 2, species_n, layers, 1, nx), f32),
                pltpu.VMEM((SUBSTEPS, 2, species_n, layers, 1, nx), f32),
                pltpu.VMEM((peers, yrows, LANES), f32),
                pltpu.VMEM((peers, yrows, LANES), f32),
                pltpu.VMEM((8, LANES), f32),
                pltpu.VMEM((peers, 8, LANES), f32),
                dma((2,)),
                dma((2,)),
                dma((SUBSTEPS, 2)),
                dma((SUBSTEPS, 2)),
                dma,
                dma,
                dma,
                dma,
            ],
            compiler_params=pltpu.CompilerParams(
                collective_id=0, has_side_effects=True, vmem_limit_bytes=VMEM_GRANT
            ),
        )(*(pltpu.with_memory_space_constraint(x, pltpu.HBM) for x in inputs))
        return outs

    slab = P("ens", "gx", None)
    stacked = P(None, "ens", "gx", None)
    in_specs = (slab, slab, slab, slab, P("ens"), slab, stacked, stacked, slab, P("ens", None))
    out_specs = (slab, stacked, stacked)
    return jax.shard_map(step, mesh=mesh, in_specs=in_specs, out_specs=out_specs, check_vma=False)
```

```python
import functools

import jax
import jax.numpy as jnp
from jax import lax
from jax.experimental import pallas as pl
from jax.experimental.pallas import tpu as pltpu
from jax.sharding import PartitionSpec as P

SUBSTEPS = 2
LANES = 128
VMEM_GRANT = 24 * 1024 * 1024
step_size = 0.5


def harmonic(left_val, right_val):
    return 2.0 * left_val * right_val / (left_val + right_val)


def iota(shape, dim):
    return lax.broadcasted_iota(jnp.int32, shape, dim)


def shift_z(field, by):
    zero = jnp.zeros_like(field[:1])
    if by > 0:
        return jnp.concatenate([field[1:], zero], axis=0)
    return jnp.concatenate([zero, field[:-1]], axis=0)


def next_lane(field):
    return pltpu.roll(field, field.shape[-1] - 1, axis=field.ndim - 1)


def last_lane(field):
    return pltpu.roll(field, 1, axis=field.ndim - 1)


def next_row(field):
    return pltpu.roll(field, field.shape[1] - 1, axis=1)


def last_row(field):
    return pltpu.roll(field, 1, axis=1)


def group_transpose(tiles, width):
    count = len(tiles)
    tiles = list(tiles)
    group = iota(tiles[0].shape, 1) // width
    half = count // 2
    while half:
        low = (group & half) == 0
        for i in range(count):
            if i & half:
                continue
            a, b = tiles[i], tiles[i + half]
            tiles[i] = jnp.where(low, a, pltpu.roll(b, half * width, axis=1))
            tiles[i + half] = jnp.where(low, pltpu.roll(a, LANES - half * width, axis=1), b)
        half //= 2
    return tiles


def kernel(
    peers,
    pres_hbm,
    src_hbm,
    perm_hbm,
    region_hbm,
    factor_hbm,
    bound_hbm,
    flux_hbm,
    conc_hbm,
    poro_hbm,
    react_hbm,
    pres_out,
    flux_out,
    spec_out,
    pres_ref,
    src_ref,
    perm_ref,
    region_ref,
    factor_ref,
    bound_ref,
    flux_ref,
    conc_ref,
    poro_ref,
    react_ref,
    load_sem,
    pack_out,
    pack_in,
    edge_out,
    edge_in,
    turn_out,
    turn_in,
    sum_out,
    sum_in,
    pack_ss,
    pack_rs,
    edge_ss,
    edge_rs,
    turn_ss,
    turn_rs,
    sum_ss,
    sum_rs,
):
    me = lax.axis_index("gx")
    layers, rows, ny = pres_ref.shape
    species_n, _, yrows, nx = conc_ref.shape
    has_low = me > 0
    has_high = me < peers - 1

    barrier = pltpu.get_barrier_semaphore()

    def greet(k, carry):
        pl.semaphore_signal(barrier, inc=1, device_id={"gx": lax.rem(me + k, peers)})
        return carry

    lax.fori_loop(1, peers, greet, 0, unroll=peers <= 16)

    pairs = (
        (region_hbm, region_ref),
        (factor_hbm, factor_ref),
        (perm_hbm, perm_ref),
        (bound_hbm, bound_ref),
        (pres_hbm, pres_ref),
        (src_hbm, src_ref),
        (flux_hbm, flux_ref),
        (conc_hbm, conc_ref),
        (poro_hbm, poro_ref),
        (react_hbm, react_ref),
    )
    loads = [pltpu.make_async_copy(a, b, load_sem.at[i]) for i, (a, b) in enumerate(pairs)]
    for load in loads:
        load.start()
    for load in loads[:6]:
        load.wait()

    region = region_ref[...]
    factor = jnp.full(region.shape, factor_ref[0], jnp.float32)
    for region_id in range(1, factor_ref.shape[0]):
        factor = jnp.where(region == region_id, factor_ref[region_id], factor)
    conduct = factor * perm_ref[...]
    field = conduct.shape
    row_id = iota(field, 1)
    first_row, end_row = row_id == 0, row_id == rows - 1
    lane_end = iota(field, 2) == ny - 1

    def y_faces(c):
        edge = iota(c.shape, 2) == ny - 1
        return jnp.where(edge, 0.0, harmonic(c, next_lane(c)))

    def z_faces(c):
        zero = jnp.zeros_like(c[:1])
        return jnp.concatenate([harmonic(c[:-1], c[1:]), zero], axis=0)

    ty = y_faces(conduct)
    ty_low = last_lane(ty)
    tz = z_faces(conduct)
    tz_low = shift_z(tz, -1)
    tx = jnp.where(end_row, 0.0, harmonic(conduct, next_row(conduct)))
    tx_low = last_row(tx)
    bound = bound_ref[...]
    leakage = jnp.where(bound == 0, 0.05, jnp.where(bound == 1, 1.0, 10.0)) * conduct
    diag_part = leakage + tx_low + tx + ty_low + ty + tz_low + tz

    def around(f):
        return (
            tx_low * last_row(f)
            + tx * next_row(f)
            + ty_low * last_lane(f)
            + ty * next_lane(f)
            + tz_low * shift_z(f, -1)
            + tz * shift_z(f, 1)
        )

    pres = pres_ref[...]
    res_part = src_ref[...] - (diag_part * pres - around(pres))
    pack_out[0, 0] = conduct[:, 0:1]
    pack_out[0, 1] = pres[:, 0:1]
    pack_out[0, 2] = res_part[:, 0:1]
    pack_out[0, 3] = diag_part[:, 0:1]
    pack_out[0, 4] = res_part[:, 1:2] / diag_part[:, 1:2]
    pack_out[0, 5] = tx[:, 0:1]
    pack_out[1, 0] = conduct[:, rows - 1 : rows]
    pack_out[1, 1] = pres[:, rows - 1 : rows]
    pack_out[1, 2] = res_part[:, rows - 1 : rows]
    pack_out[1, 3] = diag_part[:, rows - 1 : rows]

    pl.semaphore_wait(barrier, peers - 1)

    def to_side(out, into, ss, rs, side):
        return pltpu.make_async_remote_copy(
            src_ref=out,
            dst_ref=into,
            send_sem=ss,
            recv_sem=rs,
            device_id={"gx": me - 1 if side == 0 else me + 1},
        )

    def pack_copy(side):
        used = 6 if side == 0 else 4
        span = pl.ds(0, used)
        return to_side(
            pack_out.at[side, span],
            pack_in.at[1 - side, span],
            pack_ss.at[side],
            pack_rs.at[1 - side],
            side,
        )

    def edge_copy(step, side):
        return to_side(
            edge_out.at[step, side],
            edge_in.at[step, 1 - side],
            edge_ss.at[step, side],
            edge_rs.at[step, 1 - side],
            side,
        )

    def turn_copy(k):
        to = lax.rem(me + k, peers)
        return pltpu.make_async_remote_copy(
            src_ref=turn_out.at[to],
            dst_ref=turn_in.at[me],
            send_sem=turn_ss,
            recv_sem=turn_rs,
            device_id={"gx": to},
        )

    def sum_copy(k):
        to = lax.rem(me + k, peers)
        return pltpu.make_async_remote_copy(
            src_ref=sum_out,
            dst_ref=sum_in.at[me],
            send_sem=sum_ss,
            recv_sem=sum_rs,
            device_id={"gx": to},
        )

    def start_all(copy_of):
        def body(k, carry):
            copy_of(k).start()
            return carry

        lax.fori_loop(1, peers, body, 0, unroll=peers <= 16)

    def both_sides(copy_of):
        @pl.when(has_low)
        def _():
            copy_of(0).start()

        @pl.when(has_high)
        def _():
            copy_of(1).start()

    def await_sides(copy_of):
        @pl.when(has_low)
        def _():
            copy_of(1).wait_recv()

        @pl.when(has_high)
        def _():
            copy_of(0).wait_recv()

    def sent_sides(copy_of):
        @pl.when(has_low)
        def _():
            copy_of(0).wait_send()

        @pl.when(has_high)
        def _():
            copy_of(1).wait_send()

    def whole(ref_out, ref_in, ss, rs):
        return pltpu.make_async_remote_copy(
            src_ref=ref_out, dst_ref=ref_in, send_sem=ss, recv_sem=rs, device_id={"gx": me}
        )

    both_sides(pack_copy)
    for load in loads[6:]:
        load.wait()
    edge_out[0, 0] = conc_ref[:, :, 0:1, :]
    edge_out[0, 1] = conc_ref[:, :, yrows - 1 : yrows, :]

    flux_y = jnp.where(iota((layers, rows, ny), 2) == ny - 1, 0.0, flux_ref[1])
    flux_y_low = last_lane(flux_y)
    turned = jnp.concatenate([flux_ref[0], flux_y, flux_ref[2], flux_y_low], axis=0)
    turned = turned.reshape(4 * layers * rows, ny).T
    turn_out[...] = turned.reshape(peers, yrows, LANES)
    both_sides(functools.partial(edge_copy, 0))
    start_all(turn_copy)
    turn_in[me] = turn_out[me]

    await_sides(pack_copy)
    zero_row = jnp.zeros((layers, 1, ny), jnp.float32)

    def low_of(k):
        return jnp.where(has_low, pack_in[0, k], zero_row)

    def high_of(k):
        return jnp.where(has_high, pack_in[1, k], zero_row)

    one_row = jnp.ones_like(zero_row)
    cond_b = jnp.where(has_low, pack_in[0, 0], one_row)
    cond_a = jnp.where(has_high, pack_in[1, 0], one_row)
    pres_b, pres_a = low_of(1), high_of(1)
    diag_b = jnp.where(has_low, pack_in[0, 3], one_row)
    diag_a = jnp.where(has_high, pack_in[1, 3], one_row)
    t_lo = jnp.where(has_low, harmonic(cond_b, conduct[:, 0:1]), zero_row)
    t_hi = jnp.where(has_high, harmonic(conduct[:, rows - 1 : rows], cond_a), zero_row)
    drop_b = t_lo * (pres_b - pres[:, 0:1])
    drop_a = t_hi * (pres_a - pres[:, rows - 1 : rows])
    z_b = (low_of(2) - drop_b) / (diag_b + t_lo)
    full_a = diag_a + t_hi
    z_a = (high_of(2) - drop_a) / full_a

    zero = jnp.zeros(field, jnp.float32)
    diag = diag_part + jnp.where(first_row, t_lo, zero) + jnp.where(end_row, t_hi, zero)
    res = res_part + jnp.where(first_row, drop_b, zero) + jnp.where(end_row, drop_a, zero)
    z0 = res / diag
    nz = (
        around(z0)
        + jnp.where(first_row, t_lo * z_b, zero)
        + jnp.where(end_row, t_hi * z_a, zero)
    )
    v = nz / diag
    ty_a = y_faces(cond_a)
    tz_a = z_faces(cond_a)
    nz_a = (
        t_hi * z0[:, rows - 1 : rows]
        + high_of(5) * high_of(4)
        + last_lane(ty_a) * last_lane(z_a)
        + ty_a * next_lane(z_a)
        + shift_z(tz_a, -1) * shift_z(z_a, -1)
        + tz_a * shift_z(z_a, 1)
    )
    v_a = nz_a / full_a
    tx_all = jnp.where(end_row, t_hi, tx)
    v_up = tx_all * jnp.where(end_row, v_a, next_row(v)) + ty * next_lane(v) + tz * shift_z(v, 1)

    def column(f):
        f = jnp.sum(jnp.sum(f, axis=0), axis=0, keepdims=True)
        return sum(f[:, i : i + LANES] for i in range(0, ny, LANES))

    columns = (column(res * z0), column(z0 * nz), column(v * nz), column(2.0 * (v * v_up)))
    sum_row = iota((8, LANES), 0)
    partial = jnp.zeros((8, LANES), jnp.float32)
    for k, col in enumerate(columns):
        partial = jnp.where(sum_row == k, col, partial)
    sum_out[...] = partial
    start_all(sum_copy)
    sum_in[me] = partial

    some = pl.ds(0, peers - 1)
    whole(turn_out.at[some], turn_in.at[some], turn_ss, turn_rs).wait_recv()
    await_sides(functools.partial(edge_copy, 0))
    per = LANES // rows
    blocks = [
        group_transpose([turn_in[b * per + i] for i in range(per)], rows)
        for b in range(peers // per)
    ]

    def component(c):
        def layer(z):
            parts = [block[c * layers + z] for block in blocks]
            return parts[0] if len(parts) == 1 else jnp.concatenate(parts, axis=1)

        return jnp.stack([layer(z) for z in range(layers)])

    shape = (layers, yrows, nx)
    y_first, y_end = iota(shape, 1) == 0, iota(shape, 1) == yrows - 1
    f_x = jnp.where(iota(shape, 2) == nx - 1, 0.0, component(0))
    f_y = component(1)
    f_z = jnp.where(iota(shape, 0) == layers - 1, 0.0, component(2))
    f_y_low = component(3)
    up_x, up_y, up_z, up_y_low = f_x > 0, f_y > 0, f_z > 0, f_y_low > 0
    weight = step_size / poro_ref[...]
    edge_zero = jnp.zeros((layers, 1, nx), jnp.float32)

    def advance(species, step):
        result = []
        for s in range(species_n):
            c = species[s]
            below = jnp.where(has_low, edge_in[step, 0, s], edge_zero)
            above = jnp.where(has_high, edge_in[step, 1, s], edge_zero)
            c_below = jnp.where(y_first, below, last_row(c))
            c_above = jnp.where(y_end, above, next_row(c))
            div = f_y * jnp.where(up_y, c, c_above) - f_y_low * jnp.where(up_y_low, c_below, c)
            carried = f_x * jnp.where(up_x, c, next_lane(c))
            div = div + (carried - last_lane(carried))
            carried = f_z * jnp.where(up_z, c, shift_z(c, 1))
            div = div + (carried - shift_z(carried, -1))
            react = react_ref[s, 0] * species[0]
            for t in range(1, species_n):
                react = react + react_ref[s, t] * species[t]
            result.append(c - weight * div + step_size * react)
        return result

    species = advance([conc_ref[s] for s in range(species_n)], 0)
    for s in range(species_n):
        edge_out[1, 0, s] = species[s][:, 0:1]
        edge_out[1, 1, s] = species[s][:, yrows - 1 : yrows]
    both_sides(functools.partial(edge_copy, 1))

    whole(sum_in.at[some], sum_in.at[some], sum_ss, sum_rs).wait_recv()
    total = sum_in[0]
    for i in range(1, peers):
        total = total + sum_in[i]
    total = jnp.sum(total, axis=1, keepdims=True)
    g00, g01, g11, g12 = (total[k : k + 1] for k in range(4))
    delta0 = g00 - g01
    a0 = g00 / delta0
    e0 = -g01 / delta0
    gamma1 = e0 * e0 * g00 + 2.0 * a0 * e0 * g01 + a0 * a0 * g11
    cross1 = e0 * e0 * g01 + 2.0 * a0 * e0 * g11 + a0 * a0 * g12
    beta = gamma1 / g00
    a1 = gamma1 / ((gamma1 - cross1) - beta * gamma1 / a0)
    on_z = (a0 + a1 * (e0 + beta)).reshape(1, 1, 1)
    on_v = (a1 * a0).reshape(1, 1, 1)
    pressure = pres + on_z * z0 + on_v * v
    pressure_a = pres_a + on_z * z_a + on_v * v_a
    pres_out[...] = pressure
    flux_out[0] = tx_all * (pressure - jnp.where(end_row, pressure_a, next_row(pressure)))
    flux_out[1] = ty * (pressure - next_lane(pressure))
    flux_out[2] = tz * (pressure - shift_z(pressure, 1))

    await_sides(functools.partial(edge_copy, 1))
    species = advance(species, 1)
    for s in range(species_n):
        spec_out[s] = species[s]

    sent_sides(pack_copy)
    sent_sides(functools.partial(edge_copy, 0))
    sent_sides(functools.partial(edge_copy, 1))
    whole(turn_out.at[some], turn_in.at[some], turn_ss, turn_rs).wait_send()
    whole(sum_in.at[some], sum_in.at[some], sum_ss, sum_rs).wait_send()


def write_out(a, b, c, a_out, b_out, c_out, sem):
    pairs = ((c, c_out), (b, b_out), (a, a_out))
    copies = [pltpu.make_async_copy(x, y, sem.at[i]) for i, (x, y) in enumerate(pairs)]
    for copy in copies:
        copy.start()
    for copy in copies:
        copy.wait()


def solution(mesh):
    peers = mesh.shape["gx"]

    def step(pres, src, perm, region, factor, bound, flux, conc, poro, react):
        layers, rows, ny = pres.shape
        species_n, _, yrows, nx = conc.shape
        f32 = jnp.float32
        dma = pltpu.SemaphoreType.DMA
        inputs = (pres, src, perm, region, factor, bound, flux, conc, poro, react)
        hbm = pl.BlockSpec(memory_space=pltpu.HBM)
        vmem = pl.BlockSpec(memory_space=pltpu.VMEM)
        outs = pl.pallas_call(
            functools.partial(kernel, peers),
            out_shape=(
                jax.ShapeDtypeStruct(pres.shape, f32),
                jax.ShapeDtypeStruct(flux.shape, f32),
                jax.ShapeDtypeStruct(conc.shape, f32),
            ),
            in_specs=[hbm] * 10,
            out_specs=(vmem,) * 3,
            scratch_shapes=[
                pltpu.VMEM(pres.shape, f32),
                pltpu.VMEM(pres.shape, f32),
                pltpu.VMEM(pres.shape, f32),
                pltpu.VMEM(pres.shape, jnp.int32),
                pltpu.SMEM(factor.shape, f32),
                pltpu.VMEM(pres.shape, jnp.int32),
                pltpu.VMEM(flux.shape, f32),
                pltpu.VMEM(conc.shape, f32),
                pltpu.VMEM(poro.shape, f32),
                pltpu.SMEM(react.shape, f32),
                dma((10,)),
                pltpu.VMEM((2, 6, layers, 1, ny), f32),
                pltpu.VMEM((2, 6, layers, 1, ny), f32),
                pltpu.VMEM((SUBSTEPS, 2, species_n, layers, 1, nx), f32),
                pltpu.VMEM((SUBSTEPS, 2, species_n, layers, 1, nx), f32),
                pltpu.VMEM((peers, yrows, LANES), f32),
                pltpu.VMEM((peers, yrows, LANES), f32),
                pltpu.VMEM((8, LANES), f32),
                pltpu.VMEM((peers, 8, LANES), f32),
                dma((2,)),
                dma((2,)),
                dma((SUBSTEPS, 2)),
                dma((SUBSTEPS, 2)),
                dma,
                dma,
                dma,
                dma,
            ],
            compiler_params=pltpu.CompilerParams(
                collective_id=0, has_side_effects=True, vmem_limit_bytes=VMEM_GRANT
            ),
        )(*(pltpu.with_memory_space_constraint(x, pltpu.HBM) for x in inputs))
        return pl.pallas_call(
            write_out,
            out_shape=tuple(jax.ShapeDtypeStruct(o.shape, f32) for o in outs),
            in_specs=[vmem] * 3,
            out_specs=(hbm,) * 3,
            scratch_shapes=[dma((3,))],
        )(*outs)

    slab = P("ens", "gx", None)
    stacked = P(None, "ens", "gx", None)
    in_specs = (slab, slab, slab, slab, P("ens"), slab, stacked, stacked, slab, P("ens", None))
    out_specs = (slab, stacked, stacked)
    return jax.shard_map(step, mesh=mesh, in_specs=in_specs, out_specs=out_specs, check_vma=False)
```

```python
import functools

import jax
import jax.numpy as jnp
from jax import lax
from jax.experimental import pallas as pl
from jax.experimental.pallas import tpu as pltpu
from jax.sharding import PartitionSpec as P

SUBSTEPS = 2
LANES = 128
VMEM_GRANT = 24 * 1024 * 1024
step_size = 0.5


def harmonic(left_val, right_val):
    return 2.0 * left_val * right_val / (left_val + right_val)


def iota(shape, dim):
    return lax.broadcasted_iota(jnp.int32, shape, dim)


def shift_z(field, by):
    zero = jnp.zeros_like(field[:1])
    if by > 0:
        return jnp.concatenate([field[1:], zero], axis=0)
    return jnp.concatenate([zero, field[:-1]], axis=0)


def next_lane(field):
    return pltpu.roll(field, field.shape[-1] - 1, axis=field.ndim - 1)


def last_lane(field):
    return pltpu.roll(field, 1, axis=field.ndim - 1)


def next_row(field):
    return pltpu.roll(field, field.shape[1] - 1, axis=1)


def last_row(field):
    return pltpu.roll(field, 1, axis=1)


def group_transpose(tiles, width):
    count = len(tiles)
    tiles = list(tiles)
    group = iota(tiles[0].shape, 1) // width
    half = count // 2
    while half:
        low = (group & half) == 0
        for i in range(count):
            if i & half:
                continue
            a, b = tiles[i], tiles[i + half]
            tiles[i] = jnp.where(low, a, pltpu.roll(b, half * width, axis=1))
            tiles[i + half] = jnp.where(low, pltpu.roll(a, LANES - half * width, axis=1), b)
        half //= 2
    return tiles


def kernel(
    peers,
    pres_hbm,
    src_hbm,
    perm_hbm,
    region_hbm,
    factor_hbm,
    bound_hbm,
    flux_hbm,
    conc_hbm,
    poro_hbm,
    react_hbm,
    pres_out,
    flux_out,
    spec_out,
    pres_ref,
    src_ref,
    perm_ref,
    region_ref,
    factor_ref,
    bound_ref,
    flux_ref,
    conc_ref,
    poro_ref,
    react_ref,
    load_sem,
    pack_out,
    pack_in,
    edge_out,
    edge_in,
    turn_out,
    turn_in,
    sum_out,
    sum_in,
    pack_ss,
    pack_rs,
    edge_ss,
    edge_rs,
    turn_ss,
    turn_rs,
    sum_ss,
    sum_rs,
):
    me = lax.axis_index("gx")
    layers, rows, ny = pres_ref.shape
    species_n, _, yrows, nx = conc_ref.shape
    has_low = me > 0
    has_high = me < peers - 1

    barrier = pltpu.get_barrier_semaphore()

    def greet(k, carry):
        pl.semaphore_signal(barrier, inc=1, device_id={"gx": lax.rem(me + k, peers)})
        return carry

    lax.fori_loop(1, peers, greet, 0, unroll=peers <= 16)

    pairs = (
        (region_hbm, region_ref),
        (factor_hbm, factor_ref),
        (perm_hbm, perm_ref),
        (bound_hbm, bound_ref),
        (pres_hbm, pres_ref),
        (src_hbm, src_ref),
        (flux_hbm, flux_ref),
        (conc_hbm, conc_ref),
        (poro_hbm, poro_ref),
        (react_hbm, react_ref),
    )
    loads = [pltpu.make_async_copy(a, b, load_sem.at[i]) for i, (a, b) in enumerate(pairs)]
    for load in loads:
        load.start()
    for load in loads[:6]:
        load.wait()

    region = region_ref[...]
    factor = jnp.full(region.shape, factor_ref[0], jnp.float32)
    for region_id in range(1, factor_ref.shape[0]):
        factor = jnp.where(region == region_id, factor_ref[region_id], factor)
    conduct = factor * perm_ref[...]
    field = conduct.shape
    row_id = iota(field, 1)
    first_row, end_row = row_id == 0, row_id == rows - 1
    lane_end = iota(field, 2) == ny - 1

    def y_faces(c):
        edge = iota(c.shape, 2) == ny - 1
        return jnp.where(edge, 0.0, harmonic(c, next_lane(c)))

    def z_faces(c):
        zero = jnp.zeros_like(c[:1])
        return jnp.concatenate([harmonic(c[:-1], c[1:]), zero], axis=0)

    ty = y_faces(conduct)
    ty_low = last_lane(ty)
    tz = z_faces(conduct)
    tz_low = shift_z(tz, -1)
    tx = jnp.where(end_row, 0.0, harmonic(conduct, next_row(conduct)))
    tx_low = last_row(tx)
    bound = bound_ref[...]
    leakage = jnp.where(bound == 0, 0.05, jnp.where(bound == 1, 1.0, 10.0)) * conduct
    diag_part = leakage + tx_low + tx + ty_low + ty + tz_low + tz

    def around(f):
        return (
            tx_low * last_row(f)
            + tx * next_row(f)
            + ty_low * last_lane(f)
            + ty * next_lane(f)
            + tz_low * shift_z(f, -1)
            + tz * shift_z(f, 1)
        )

    pres = pres_ref[...]
    res_part = src_ref[...] - (diag_part * pres - around(pres))
    pack_out[0, 0] = conduct[:, 0:1]
    pack_out[0, 1] = pres[:, 0:1]
    pack_out[0, 2] = res_part[:, 0:1]
    pack_out[0, 3] = diag_part[:, 0:1]
    pack_out[0, 4] = res_part[:, 1:2] / diag_part[:, 1:2]
    pack_out[0, 5] = tx[:, 0:1]
    pack_out[1, 0] = conduct[:, rows - 1 : rows]
    pack_out[1, 1] = pres[:, rows - 1 : rows]
    pack_out[1, 2] = res_part[:, rows - 1 : rows]
    pack_out[1, 3] = diag_part[:, rows - 1 : rows]

    pl.semaphore_wait(barrier, peers - 1)

    def to_side(out, into, ss, rs, side):
        return pltpu.make_async_remote_copy(
            src_ref=out,
            dst_ref=into,
            send_sem=ss,
            recv_sem=rs,
            device_id={"gx": me - 1 if side == 0 else me + 1},
        )

    def pack_copy(side):
        used = 6 if side == 0 else 4
        span = pl.ds(0, used)
        return to_side(
            pack_out.at[side, span],
            pack_in.at[1 - side, span],
            pack_ss.at[side],
            pack_rs.at[1 - side],
            side,
        )

    def edge_copy(step, side):
        return to_side(
            edge_out.at[step, side],
            edge_in.at[step, 1 - side],
            edge_ss.at[step, side],
            edge_rs.at[step, 1 - side],
            side,
        )

    def turn_copy(k):
        to = lax.rem(me + k, peers)
        return pltpu.make_async_remote_copy(
            src_ref=turn_out.at[to],
            dst_ref=turn_in.at[me],
            send_sem=turn_ss,
            recv_sem=turn_rs,
            device_id={"gx": to},
        )

    def sum_copy(k):
        to = lax.rem(me + k, peers)
        return pltpu.make_async_remote_copy(
            src_ref=sum_out,
            dst_ref=sum_in.at[me],
            send_sem=sum_ss,
            recv_sem=sum_rs,
            device_id={"gx": to},
        )

    def start_all(copy_of):
        def body(k, carry):
            copy_of(k).start()
            return carry

        lax.fori_loop(1, peers, body, 0, unroll=peers <= 16)

    def both_sides(copy_of):
        @pl.when(has_low)
        def _():
            copy_of(0).start()

        @pl.when(has_high)
        def _():
            copy_of(1).start()

    def await_sides(copy_of):
        @pl.when(has_low)
        def _():
            copy_of(1).wait_recv()

        @pl.when(has_high)
        def _():
            copy_of(0).wait_recv()

    def sent_sides(copy_of):
        @pl.when(has_low)
        def _():
            copy_of(0).wait_send()

        @pl.when(has_high)
        def _():
            copy_of(1).wait_send()

    def whole(ref_out, ref_in, ss, rs):
        return pltpu.make_async_remote_copy(
            src_ref=ref_out, dst_ref=ref_in, send_sem=ss, recv_sem=rs, device_id={"gx": me}
        )

    both_sides(pack_copy)
    for load in loads[6:]:
        load.wait()
    edge_out[0, 0] = conc_ref[:, :, 0:1, :]
    edge_out[0, 1] = conc_ref[:, :, yrows - 1 : yrows, :]

    flux_y = jnp.where(iota((layers, rows, ny), 2) == ny - 1, 0.0, flux_ref[1])
    flux_y_low = last_lane(flux_y)
    turned = jnp.concatenate([flux_ref[0], flux_y, flux_ref[2], flux_y_low], axis=0)
    turned = turned.reshape(4 * layers * rows, ny).T
    turn_out[...] = turned.reshape(peers, yrows, LANES)
    both_sides(functools.partial(edge_copy, 0))
    start_all(turn_copy)
    turn_in[me] = turn_out[me]

    await_sides(pack_copy)
    zero_row = jnp.zeros((layers, 1, ny), jnp.float32)

    def low_of(k):
        return jnp.where(has_low, pack_in[0, k], zero_row)

    def high_of(k):
        return jnp.where(has_high, pack_in[1, k], zero_row)

    one_row = jnp.ones_like(zero_row)
    cond_b = jnp.where(has_low, pack_in[0, 0], one_row)
    cond_a = jnp.where(has_high, pack_in[1, 0], one_row)
    pres_b, pres_a = low_of(1), high_of(1)
    diag_b = jnp.where(has_low, pack_in[0, 3], one_row)
    diag_a = jnp.where(has_high, pack_in[1, 3], one_row)
    t_lo = jnp.where(has_low, harmonic(cond_b, conduct[:, 0:1]), zero_row)
    t_hi = jnp.where(has_high, harmonic(conduct[:, rows - 1 : rows], cond_a), zero_row)
    drop_b = t_lo * (pres_b - pres[:, 0:1])
    drop_a = t_hi * (pres_a - pres[:, rows - 1 : rows])
    z_b = (low_of(2) - drop_b) / (diag_b + t_lo)
    full_a = diag_a + t_hi
    z_a = (high_of(2) - drop_a) / full_a

    zero = jnp.zeros(field, jnp.float32)
    diag = diag_part + jnp.where(first_row, t_lo, zero) + jnp.where(end_row, t_hi, zero)
    res = res_part + jnp.where(first_row, drop_b, zero) + jnp.where(end_row, drop_a, zero)
    z0 = res / diag
    nz = (
        around(z0)
        + jnp.where(first_row, t_lo * z_b, zero)
        + jnp.where(end_row, t_hi * z_a, zero)
    )
    v = nz / diag
    ty_a = y_faces(cond_a)
    tz_a = z_faces(cond_a)
    nz_a = (
        t_hi * z0[:, rows - 1 : rows]
        + high_of(5) * high_of(4)
        + last_lane(ty_a) * last_lane(z_a)
        + ty_a * next_lane(z_a)
        + shift_z(tz_a, -1) * shift_z(z_a, -1)
        + tz_a * shift_z(z_a, 1)
    )
    v_a = nz_a / full_a
    tx_all = jnp.where(end_row, t_hi, tx)
    v_up = tx_all * jnp.where(end_row, v_a, next_row(v)) + ty * next_lane(v) + tz * shift_z(v, 1)

    def column(f):
        f = jnp.sum(jnp.sum(f, axis=0), axis=0, keepdims=True)
        return sum(f[:, i : i + LANES] for i in range(0, ny, LANES))

    columns = (column(res * z0), column(z0 * nz), column(v * nz), column(2.0 * (v * v_up)))
    sum_row = iota((8, LANES), 0)
    partial = jnp.zeros((8, LANES), jnp.float32)
    for k, col in enumerate(columns):
        partial = jnp.where(sum_row == k, col, partial)
    sum_out[...] = partial
    start_all(sum_copy)
    sum_in[me] = partial

    some = pl.ds(0, peers - 1)
    whole(turn_out.at[some], turn_in.at[some], turn_ss, turn_rs).wait_recv()
    await_sides(functools.partial(edge_copy, 0))
    per = LANES // rows
    blocks = [
        group_transpose([turn_in[b * per + i] for i in range(per)], rows)
        for b in range(peers // per)
    ]

    def component(c):
        def layer(z):
            parts = [block[c * layers + z] for block in blocks]
            return parts[0] if len(parts) == 1 else jnp.concatenate(parts, axis=1)

        return jnp.stack([layer(z) for z in range(layers)])

    shape = (layers, yrows, nx)
    y_first, y_end = iota(shape, 1) == 0, iota(shape, 1) == yrows - 1
    f_x = jnp.where(iota(shape, 2) == nx - 1, 0.0, component(0))
    f_y = component(1)
    f_z = jnp.where(iota(shape, 0) == layers - 1, 0.0, component(2))
    f_y_low = component(3)
    up_x, up_y, up_z, up_y_low = f_x > 0, f_y > 0, f_z > 0, f_y_low > 0
    weight = step_size / poro_ref[...]
    edge_zero = jnp.zeros((layers, 1, nx), jnp.float32)

    def advance(species, step):
        result = []
        for s in range(species_n):
            c = species[s]
            below = jnp.where(has_low, edge_in[step, 0, s], edge_zero)
            above = jnp.where(has_high, edge_in[step, 1, s], edge_zero)
            c_below = jnp.where(y_first, below, last_row(c))
            c_above = jnp.where(y_end, above, next_row(c))
            div = f_y * jnp.where(up_y, c, c_above) - f_y_low * jnp.where(up_y_low, c_below, c)
            carried = f_x * jnp.where(up_x, c, next_lane(c))
            div = div + (carried - last_lane(carried))
            carried = f_z * jnp.where(up_z, c, shift_z(c, 1))
            div = div + (carried - shift_z(carried, -1))
            react = react_ref[s, 0] * species[0]
            for t in range(1, species_n):
                react = react + react_ref[s, t] * species[t]
            result.append(c - weight * div + step_size * react)
        return result

    species = advance([conc_ref[s] for s in range(species_n)], 0)
    for s in range(species_n):
        edge_out[1, 0, s] = species[s][:, 0:1]
        edge_out[1, 1, s] = species[s][:, yrows - 1 : yrows]
    both_sides(functools.partial(edge_copy, 1))

    whole(sum_in.at[some], sum_in.at[some], sum_ss, sum_rs).wait_recv()
    total = sum_in[0]
    for i in range(1, peers):
        total = total + sum_in[i]
    total = jnp.sum(total, axis=1, keepdims=True)
    g00, g01, g11, g12 = (total[k : k + 1] for k in range(4))
    delta0 = g00 - g01
    a0 = g00 / delta0
    e0 = -g01 / delta0
    gamma1 = e0 * e0 * g00 + 2.0 * a0 * e0 * g01 + a0 * a0 * g11
    cross1 = e0 * e0 * g01 + 2.0 * a0 * e0 * g11 + a0 * a0 * g12
    beta = gamma1 / g00
    a1 = gamma1 / ((gamma1 - cross1) - beta * gamma1 / a0)
    on_z = (a0 + a1 * (e0 + beta)).reshape(1, 1, 1)
    on_v = (a1 * a0).reshape(1, 1, 1)
    pressure = pres + on_z * z0 + on_v * v
    pressure_a = pres_a + on_z * z_a + on_v * v_a
    pres_out[...] = pressure
    flux_out[0] = tx_all * (pressure - jnp.where(end_row, pressure_a, next_row(pressure)))
    flux_out[1] = ty * (pressure - next_lane(pressure))
    flux_out[2] = tz * (pressure - shift_z(pressure, 1))

    await_sides(functools.partial(edge_copy, 1))
    species = advance(species, 1)
    for s in range(species_n):
        spec_out[s] = species[s]

    sent_sides(pack_copy)
    sent_sides(functools.partial(edge_copy, 0))
    sent_sides(functools.partial(edge_copy, 1))
    whole(turn_out.at[some], turn_in.at[some], turn_ss, turn_rs).wait_send()
    whole(sum_in.at[some], sum_in.at[some], sum_ss, sum_rs).wait_send()


def solution(mesh):
    peers = mesh.shape["gx"]

    def step(pres, src, perm, region, factor, bound, flux, conc, poro, react):
        layers, rows, ny = pres.shape
        species_n, _, yrows, nx = conc.shape
        f32 = jnp.float32
        dma = pltpu.SemaphoreType.DMA
        inputs = (pres, src, perm, region, factor, bound, flux, conc, poro, react)
        hbm = pl.BlockSpec(memory_space=pltpu.HBM)
        vmem = pl.BlockSpec(memory_space=pltpu.VMEM)
        outs = pl.pallas_call(
            functools.partial(kernel, peers),
            out_shape=(
                jax.ShapeDtypeStruct(pres.shape, f32),
                jax.ShapeDtypeStruct(flux.shape, f32),
                jax.ShapeDtypeStruct(conc.shape, f32),
            ),
            in_specs=[hbm] * 10,
            out_specs=(vmem,) * 3,
            scratch_shapes=[
                pltpu.VMEM(pres.shape, f32),
                pltpu.VMEM(pres.shape, f32),
                pltpu.VMEM(pres.shape, f32),
                pltpu.VMEM(pres.shape, jnp.int32),
                pltpu.SMEM(factor.shape, f32),
                pltpu.VMEM(pres.shape, jnp.int32),
                pltpu.VMEM(flux.shape, f32),
                pltpu.VMEM(conc.shape, f32),
                pltpu.VMEM(poro.shape, f32),
                pltpu.SMEM(react.shape, f32),
                dma((10,)),
                pltpu.VMEM((2, 6, layers, 1, ny), f32),
                pltpu.VMEM((2, 6, layers, 1, ny), f32),
                pltpu.VMEM((SUBSTEPS, 2, species_n, layers, 1, nx), f32),
                pltpu.VMEM((SUBSTEPS, 2, species_n, layers, 1, nx), f32),
                pltpu.VMEM((peers, yrows, LANES), f32),
                pltpu.VMEM((peers, yrows, LANES), f32),
                pltpu.VMEM((8, LANES), f32),
                pltpu.VMEM((peers, 8, LANES), f32),
                dma((2,)),
                dma((2,)),
                dma((SUBSTEPS, 2)),
                dma((SUBSTEPS, 2)),
                dma,
                dma,
                dma,
                dma,
            ],
            compiler_params=pltpu.CompilerParams(
                collective_id=0, has_side_effects=True, vmem_limit_bytes=VMEM_GRANT
            ),
        )(*(pltpu.with_memory_space_constraint(x, pltpu.HBM) for x in inputs))
        return outs

    slab = P("ens", "gx", None)
    stacked = P(None, "ens", "gx", None)
    in_specs = (slab, slab, slab, slab, P("ens"), slab, stacked, stacked, slab, P("ens", None))
    out_specs = (slab, stacked, stacked)
    return jax.shard_map(step, mesh=mesh, in_specs=in_specs, out_specs=out_specs, check_vma=False)
```
